32 devices in a mesh: dp: 4 (over z), seq: 8 (over y, x, core).
Axes of the slice: x: 2, y: 2, z: 4, core: 2. Of those that a mesh axis runs over, the one named last changes fastest.
Arguments:
- inputs: bfloat16 [8, 1024, 768], P('dp', 'seq'), may hold values from -6 to 6
- lengths: int32 [8, 4], P('dp'), may hold values from 1 to 1024, as said below
- ln1_gain: float32 [768], replicated, may hold values from 0.5 to 1.5
- ln1_bias: float32 [768], replicated, may hold values from -3 to 3
- value_weight: bfloat16 [768, 768], replicated, may hold values from -0.21875 to 0.21875
- out_weight: bfloat16 [768, 768], replicated, may hold values from -1.25 to 1.25
- out_bias: float32 [768], replicated, may hold values from -3 to 3
- ln2_gain: float32 [768], replicated, may hold values from 0.5 to 1.5
- ln2_bias: float32 [768], replicated, may hold values from -3 to 3
- up_weight: bfloat16 [768, 3072], replicated, may hold values from -0.21875 to 0.21875
- up_bias: float32 [3072], replicated, may hold values from -3 to 3
- down_weight: bfloat16 [3072, 768], replicated, may hold values from -0.109375 to 0.109375
- down_bias: float32 [768], replicated, may hold values from -3 to 3
- logit_table: bfloat16 [12, 1024, 1024], P(None, 'seq'), may hold values from -9 to 9
- cotangent: bfloat16 [8, 1024, 768], P('dp', 'seq'), may hold values from -6 to 6
Outputs:
- layer_out: bfloat16 [8, 1024, 768], P('dp', 'seq')
- input_grad: float32 [8, 1024, 768], P('dp', 'seq')
- ln1_gain_grad: float32 [768], P('seq')
- ln1_bias_grad: float32 [768], P('seq')
- value_weight_grad: float32 [768, 768], P('seq')
- out_weight_grad: float32 [768, 768], P('seq')
- out_bias_grad: float32 [768], P('seq')
- ln2_gain_grad: float32 [768], P('seq')
- ln2_bias_grad: float32 [768], P('seq')
- up_weight_grad: float32 [768, 3072], P(None, 'seq')
- up_bias_grad: float32 [3072], P('seq')
- down_weight_grad: float32 [3072, 768], P('seq')
- down_bias_grad: float32 [768], P('seq')
- logit_grad: float32 [12, 1024, 1024], P(None, 'seq')
The draws below stay inside these ranges and needn't reach their ends.
Inputs may be any that keep to these rules, and one draw needn't show every extreme that they name: Each row's 4 lengths sum to 1024.
All inputs are finite; a program needn't handle non-finite values.
Results may differ from the reference program's by a relative error of at most 0.02.
Values may be sent and summed in bfloat16 or wider, within the bound.
No kernel may reach another device: no remote copies, remote signals or barrier semaphores. Data moves between devices by JAX's collectives and lax.ppermute only.
A program may use at most 192 MiB of HBM per device.

```python
import jax
import jax.numpy as jnp
from jax import lax

D = 768
H = 12
E = 64
FF = 3072
SEQ_DEV = 128
ROWS_DEV = 2
SEGS = 4
L = 1024
ROWS = 8


def draw_lengths(key, part):
    key = jax.random.fold_in(key, 7)
    key_cuts, key_small, key_pick = jax.random.split(key, 3)
    cuts = jnp.sort(jax.random.randint(key_cuts, (ROWS, SEGS - 1), 0, L - SEGS + 1), axis=1)
    edges = jnp.concatenate([jnp.zeros((ROWS, 1), jnp.int32), cuts, jnp.full((ROWS, 1), L - SEGS, jnp.int32)], axis=1)
    drawn = edges[:, 1:] - edges[:, :-1] + 1
    small = jax.random.randint(key_small, (ROWS, 3), 1, max(2, SEQ_DEV // 4 + 1))
    middle = L - jnp.sum(small, axis=1)
    spanning = jnp.stack([small[:, 0], middle, small[:, 1], small[:, 2]], axis=1)
    picked = jax.random.randint(key_pick, (ROWS // ROWS_DEV,), 0, ROWS_DEV)
    chosen = jnp.arange(ROWS) % ROWS_DEV == jnp.repeat(picked, ROWS_DEV)
    return jnp.where(chosen[:, None], spanning, drawn).astype(jnp.int32)


def levels(own_key, dims, shards, least, high):
    loudness, own = 1.0, jax.random.fold_in(own_key, 6)
    for axis_at, parts in shards:
        draws = jnp.exp(jax.random.uniform(jax.random.fold_in(own, axis_at), (parts,), jnp.float32, least / len(shards), high / len(shards)))
        loudness = loudness * jnp.repeat(draws, dims[axis_at] // parts).reshape([-1 if axis == axis_at else 1 for axis in range(len(dims))])
    return loudness


def scatter_about(own_key, extent, width, reach, cuts=(), kind=jnp.bfloat16):
    factor_of = levels(own_key, extent, cuts, -0.22, 0.18) if cuts else 1.0
    array = jax.random.normal(own_key, extent, jnp.float32) * width * factor_of
    return jnp.minimum(jnp.maximum(array, -reach), reach).astype(kind)


def setup_inputs(seed: int = 0) -> dict:
    key_list = jax.random.split(jax.random.key(seed), 16)
    return {
        "inputs": scatter_about(key_list[0], (ROWS, L, D), 1.0, 6.0, ((0, 4), (1, 8))),
        "lengths": draw_lengths(jax.random.fold_in(key_list[15], 71), 0),
        "ln1_gain": jnp.clip(1.0 + 0.1 * jax.random.normal(key_list[2], (D,), jnp.float32), 0.5, 1.5),
        "ln1_bias": scatter_about(key_list[3], (D,), 0.3, 3.0, (), jnp.float32),
        "value_weight": scatter_about(key_list[4], (D, D), D ** -0.5, 0.21875),
        "out_weight": scatter_about(key_list[5], (D, D), (D // 32) ** -0.5, 1.25),
        "out_bias": scatter_about(key_list[6], (D,), 0.3, 3.0, (), jnp.float32),
        "ln2_gain": jnp.clip(1.0 + 0.1 * jax.random.normal(key_list[7], (D,), jnp.float32), 0.5, 1.5),
        "ln2_bias": scatter_about(key_list[8], (D,), 0.3, 3.0, (), jnp.float32),
        "up_weight": scatter_about(key_list[9], (D, FF), D ** -0.5, 0.21875),
        "up_bias": scatter_about(key_list[10], (FF,), 0.3, 3.0, (), jnp.float32),
        "down_weight": scatter_about(key_list[11], (FF, D), FF ** -0.5, 0.109375),
        "down_bias": scatter_about(key_list[12], (D,), 0.3, 3.0, (), jnp.float32),
        "logit_table": scatter_about(key_list[13], (H, L, L), 1.5, 9.0, ((1, 8),)),
        "cotangent": scatter_about(key_list[14], (ROWS, L, D), 1.0, 6.0, ((0, 4), (1, 8))),
    }


@jax.custom_vjp
def low(v):
    return lax.optimization_barrier(v.astype(jnp.bfloat16)).astype(jnp.float32)

@jax.custom_vjp
def low_back(v):
    return v

def low_keep(v):
    return (low(v), None)

def low_pass(kept, grad):
    return (grad,)

def back_keep(v):
    return (v, None)

def back_low(kept, grad):
    return (low(grad),)
low.defvjp(low_keep, low_pass)
low_back.defvjp(back_keep, back_low)
EPSILON = 1e-05
NEGATIVE = -1e+30

def product(left, right):
    return jnp.dot(left, right, precision=lax.Precision.HIGHEST, preferred_element_type=jnp.float32)

def layer_norm(values_in, gain, bias):
    center = values_in - lax.optimization_barrier(jnp.mean(values_in, axis=-1, keepdims=True))
    variance = lax.optimization_barrier(jnp.mean(center * center, axis=-1, keepdims=True))
    return center * lax.rsqrt(variance + EPSILON) * gain + bias

def segment_info(lengths, places):
    ends = jnp.cumsum(lengths, axis=1).astype(jnp.int32)
    done = places[None, :, None] >= ends[:, None, :]
    seg_ids = lax.optimization_barrier(jnp.sum(done.astype(jnp.int32), axis=2)).astype(jnp.int32)
    start = lax.optimization_barrier(jnp.sum(jnp.where(done, lengths[:, None, :], 0), axis=2)).astype(jnp.int32)
    return (seg_ids, (places[None, :] - start).astype(jnp.int32))

def row_layer(params, row_in, row_lengths):
    ln1_gain, ln1_bias, value_weight, out_weight, out_bias, ln2_gain, ln2_bias, up_weight, up_bias, down_weight, down_bias, logit_table = params
    places = jnp.arange(L, dtype=jnp.int32)
    seg_ids, relative = segment_info(row_lengths[None, :], places)
    seg_ids = seg_ids[0]
    relative = relative[0]
    blocks = L // SEQ_DEV
    first = low(layer_norm(row_in, ln1_gain, ln1_bias))
    values = low(low_back(product(first, value_weight))).reshape(L, H, E)
    copies = low_back(jnp.broadcast_to(values[None], (blocks, L, H, E)))
    columns = logit_table[:, :, relative]
    allowed = (seg_ids[:, None] == seg_ids[None, :])[None]
    row_max = lax.optimization_barrier(jnp.max(jnp.where(allowed, columns, NEGATIVE), axis=2, keepdims=True))
    scaled = jnp.where(allowed, jnp.exp(columns - row_max), 0.0)
    row_total = lax.optimization_barrier(jnp.sum(scaled, axis=2))
    scaled_low = low(scaled).reshape(H, blocks, SEQ_DEV, L)
    weighted = low_back(jnp.einsum('hjqk,jkhe->jqhe', scaled_low, copies, precision=lax.Precision.HIGHEST).reshape(L, H, E))
    attended = low((weighted / row_total.T[:, :, None]).reshape(L, D))
    hidden1 = row_in + low_back(product(attended, out_weight) + out_bias)
    second = low(layer_norm(hidden1, ln2_gain, ln2_bias))
    pre_act = low_back(product(second, up_weight) + up_bias)
    act_low = low(jax.nn.gelu(pre_act, approximate=True))
    return hidden1 + product(act_low, down_weight) + down_bias

def reference(inputs, lengths, ln1_gain, ln1_bias, value_weight, out_weight, out_bias, ln2_gain, ln2_bias, up_weight, up_bias, down_weight, down_bias, logit_table, cotangent):
    params = tuple((p.astype(jnp.float32) for p in (ln1_gain, ln1_bias, value_weight, out_weight, out_bias, ln2_gain, ln2_bias, up_weight, up_bias, down_weight, down_bias, logit_table)))
    inputs_f = inputs.astype(jnp.float32)

    def forward(rows_in, weights):

        def step(carry, item):
            return (carry, jax.checkpoint(row_layer)(weights, item[0], item[1]))
        unused, outputs = lax.scan(step, jnp.float32(0.0), (rows_in, lengths))
        return outputs
    result, pullback = jax.vjp(forward, inputs_f, params)
    input_grad, grads = pullback(cotangent.astype(jnp.float32))
    return (result.astype(jnp.bfloat16), input_grad, grads[0], grads[1], grads[2], grads[3], grads[4], grads[5], grads[6], grads[7], grads[8], grads[9], grads[10], grads[11])
```

```python
import math

import jax
import jax.numpy as jnp
from jax import lax
from jax.experimental import pallas as pl
from jax.experimental.pallas import tpu as pltpu
from jax.sharding import PartitionSpec as P

EPSILON = 1e-05
CHUNK = 256
LANES = 128
HALF = 64
GELU_SCALE = math.sqrt(2.0 / math.pi)
GELU_CUBE = 0.044715
MIB = 1024 * 1024
COST_SCALE = 0.05
EXTRA = 32
F32 = jnp.float32
BF16 = jnp.bfloat16


def params(mib, semantics=None):
    return pltpu.CompilerParams(vmem_limit_bytes=mib * MIB, dimension_semantics=semantics)


def whole():
    return pl.BlockSpec(memory_space=pltpu.VMEM)


def smem():
    return pl.BlockSpec(memory_space=pltpu.SMEM)


def anywhere():
    return pl.BlockSpec(memory_space=pl.ANY)


def cost(flops, nbytes):
    return pl.CostEstimate(
        flops=int(flops * COST_SCALE), bytes_accessed=int(nbytes * COST_SCALE), transcendentals=0
    )


def dot(left, right):
    return jnp.dot(left, right, preferred_element_type=F32)


def dot_nt(left, right):
    return lax.dot_general(left, right, (((1,), (1,)), ((), ())), preferred_element_type=F32)


def dot_tn(left, right):
    return lax.dot_general(left, right, (((0,), (0,)), ((), ())), preferred_element_type=F32)


def low_lanes(shape):
    lane = lax.broadcasted_iota(jnp.int32, shape, len(shape) - 1)
    return lax.rem(lane, LANES) < HALF


def standardize(values_in):
    center = values_in - jnp.mean(values_in, axis=-1, keepdims=True)
    inverse = lax.rsqrt(jnp.mean(center * center, axis=-1, keepdims=True) + EPSILON)
    return (center * inverse, inverse)


def norm_backward(upstream, normed, inverse):
    return inverse * (
        upstream
        - jnp.mean(upstream, axis=-1, keepdims=True)
        - normed * jnp.mean(upstream * normed, axis=-1, keepdims=True)
    )


def pair_rows(row0, row1, store):
    count = row0.shape[1] // LANES
    low = low_lanes((row0.shape[0], LANES))
    for at in range(count):
        part0 = row0[:, at * LANES : (at + 1) * LANES]
        part1 = row1[:, at * LANES : (at + 1) * LANES]
        store(2 * at, jnp.where(low, part0, pltpu.roll(part1, HALF, 1)))
        store(2 * at + 1, jnp.where(low, pltpu.roll(part0, HALF, 1), part1))


def unpair_rows(load, heads, store):
    for at in range(heads // 2):
        even, odd = load(2 * at), load(2 * at + 1)
        low = low_lanes(even.shape)
        store(0, at, jnp.where(low, even, pltpu.roll(odd, HALF, 1)))
        store(1, at, jnp.where(low, pltpu.roll(even, HALF, 1), odd))


def segment_bounds(lens_ref, base, index, segs):
    start = jnp.int32(0)
    for at in range(segs):
        start = start + jnp.where(at < index, lens_ref[base + at], 0)
    return (start, lens_ref[base + index])


def shift_tile(source_ref, first_key, lane_start, lane_count, chunk_start, length):
    total = source_ref.shape[0]
    pieces = []
    for part in range(CHUNK // LANES):
        key = first_key + part * LANES
        window = jnp.minimum((key // LANES) * LANES, total - 2 * LANES)
        window = pl.multiple_of(window, LANES)
        row = lax.broadcasted_iota(jnp.int32, (LANES, 2 * LANES), 0)
        column = lax.broadcasted_iota(jnp.int32, (LANES, 2 * LANES), 1)
        hit = (column == row + (key - window)) & (row + (chunk_start + part * LANES) < length)
        pieces.append(
            dot(
                hit.astype(F32).astype(BF16),
                source_ref[pl.ds(window, 2 * LANES), pl.ds(lane_start, lane_count)],
            )
        )
    return jnp.concatenate(pieces, axis=0)


def prep_kernel(groups, meta_ref, x_ref, gain_ref, bias_ref, weight_ref, first_ref, low_ref, high_ref, share_ref, v2_ref):
    rows, span, width = x_ref.shape
    xhat, unused = standardize(x_ref[...].reshape(rows * span, width).astype(F32))
    first = (xhat * gain_ref[...] + bias_ref[...]).astype(BF16)
    first_ref[...] = first
    values = dot(first, weight_ref[...])

    def store(head, piece):
        v2_ref[:, head * LANES : (head + 1) * LANES] = piece.astype(BF16)

    pair_rows(values[:span], values[span:], store)
    low_ref[...] = v2_ref[:, :width]
    high_ref[...] = v2_ref[:, width:]
    part = 2 * width // groups
    for turn in range(groups):
        owner = lax.rem(meta_ref[0] + turn, groups)
        share_ref[turn] = v2_ref[:, pl.ds(pl.multiple_of(owner * part, LANES), part)]


def exp_kernel(table_ref, e_ref, et_ref):
    chunks = e_ref.shape[0]
    weights = jnp.exp(table_ref[0].astype(F32))
    for at in range(chunks):
        piece = weights[:, at * CHUNK : (at + 1) * CHUNK]
        e_ref[at, 0] = piece.astype(BF16)
        et_ref[at, 0] = piece.T.astype(BF16)


def attend_kernel(
    heads, segs, order, meta_ref, x_ref, outw_ref, outb_ref, gain_ref, bias_ref, e_hbm, *rest
):
    count = len(order)
    blocks = rest[: 2 * count]
    att_low_ref, att_ref, tot_ref, h1_ref, second_ref = rest[2 * count : 2 * count + 5]
    e_ref, values_ref, aug_ref, acc_ref, res_ref, sems = rest[2 * count + 5 :]
    rows, span, width = x_ref.shape
    here = meta_ref[rows * segs]
    copies = []
    for at, offset in enumerate(order):
        place = pl.multiple_of((here ^ offset) * span, LANES)
        for side in range(2):
            copy = pltpu.make_async_copy(
                blocks[2 * at + side],
                values_ref.at[pl.ds(place, span), pl.ds(side * width, width)],
                sems.at[2 * at + side],
            )
            copy.start()
            copies.append(copy)
    e_copy = pltpu.make_async_copy(e_hbm, e_ref, sems.at[2 * count])
    e_copy.start()
    for copy in copies:
        copy.wait()
    e_copy.wait()
    res_ref[...] = jnp.zeros_like(res_ref)
    places = here * span + lax.broadcasted_iota(jnp.int32, (span, LANES), 0)

    def one(turn, carry):
        row, index = turn // segs, lax.rem(turn, segs)
        start, length = segment_bounds(meta_ref, row * segs, index, segs)
        end = start + length

        @pl.when((start < (here + 1) * span) & (end > here * span))
        def _():
            acc_ref[...] = jnp.zeros_like(acc_ref)

            def chunk(at, state):
                moved = shift_tile(values_ref, start + at * CHUNK, 0, 2 * width, at * CHUNK, length)
                lane = lax.rem(lax.broadcasted_iota(jnp.int32, moved.shape, 1), LANES)
                within = lax.broadcasted_iota(jnp.int32, moved.shape, 0) + at * CHUNK < length
                own = (lane // HALF) == row
                aug_ref[...] = jnp.where(own, moved, within.astype(F32)).astype(BF16)
                for head in range(heads):
                    acc_ref[head] += dot(
                        e_ref[at, head], aug_ref[:, head * LANES : (head + 1) * LANES]
                    )
                return state

            lax.fori_loop(0, (length + CHUNK - 1) // CHUNK, chunk, 0)
            inside = (places >= start) & (places < end)
            res_ref[row] = jnp.where(inside[None], acc_ref[...], res_ref[row])

        return carry

    lax.fori_loop(0, rows * segs, one, 0)
    low = low_lanes((span, LANES))

    def numer(head):
        return jnp.where(low, res_ref[0, head], res_ref[1, head])

    def total(head):
        return pltpu.roll(jnp.where(low, res_ref[1, head], res_ref[0, head]), HALF, 1)

    def store_total(row, at, piece):
        tot_ref[row * span : (row + 1) * span, at * LANES : (at + 1) * LANES] = piece

    def store_att(row, at, piece):
        att_ref[row * span : (row + 1) * span, at * LANES : (at + 1) * LANES] = piece

    unpair_rows(total, heads, store_total)
    unpair_rows(numer, heads, store_att)
    attended = att_ref[...] / tot_ref[...]
    att_ref[...] = attended
    att_low = attended.astype(BF16)
    att_low_ref[...] = att_low
    hidden = (
        x_ref[...].reshape(rows * span, width).astype(F32)
        + dot(att_low, outw_ref[...])
        + outb_ref[...]
    )
    h1_ref[...] = hidden
    xhat, unused = standardize(hidden)
    second_ref[...] = (xhat * gain_ref[...] + bias_ref[...]).astype(BF16)


def ffn_kernel(
    heads,
    groups,
    span,
    meta_ref,
    second_ref,
    h1_ref,
    g_ref,
    up_ref,
    upb_ref,
    down_ref,
    downb_ref,
    outw_ref,
    gain_ref,
    att_ref,
    tot_ref,
    layer_ref,
    act_ref,
    pre_grad_ref,
    upb_grad_ref,
    h1_grad_ref,
    branch_ref,
    share_ref,
    own_ref,
    small_ref,
    back_ref,
    sum_ref,
):
    step = pl.program_id(0)
    tokens, width = h1_ref.shape

    @pl.when(step == 0)
    def _():
        back_ref[...] = jnp.zeros_like(back_ref)
        sum_ref[...] = jnp.zeros_like(sum_ref)

    up = up_ref[...]
    down = down_ref[...]
    g = g_ref[...]
    pre = dot(second_ref[...], up) + upb_ref[...]
    square = pre * pre
    bent = jnp.tanh(GELU_SCALE * (pre * (1.0 + GELU_CUBE * square)))
    half = 0.5 * (1.0 + bent)
    act = (pre * half).astype(BF16)
    act_ref[...] = act
    slope = half + 0.5 * pre * (1.0 - bent * bent) * (
        GELU_SCALE * (1.0 + 3.0 * GELU_CUBE * square)
    )
    pre_grad = (dot_nt(g, down) * slope).astype(BF16)
    pre_grad_ref[...] = pre_grad
    upb_grad_ref[...] = jnp.sum(pre_grad.astype(F32), axis=0, keepdims=True)
    back_ref[...] += dot_nt(pre_grad, up)
    sum_ref[...] += dot(act, down)

    @pl.when(step == pl.num_programs(0) - 1)
    def _():
        hidden = h1_ref[...]
        layer_ref[...] = (hidden + sum_ref[...] + downb_ref[...]).astype(BF16)
        back = back_ref[...]
        xhat, inverse = standardize(hidden)
        wide = g.astype(F32)
        hidden_grad = wide + norm_backward(back * gain_ref[...], xhat, inverse)
        h1_grad_ref[...] = hidden_grad
        branch = hidden_grad.astype(BF16)
        branch_ref[...] = branch
        small_ref[...] = jnp.zeros_like(small_ref)
        small_ref[0:1] = jnp.sum(wide, axis=0, keepdims=True)
        small_ref[1:2] = jnp.sum(back * xhat, axis=0, keepdims=True)
        small_ref[2:3] = jnp.sum(back, axis=0, keepdims=True)
        small_ref[3:4] = jnp.sum(branch.astype(F32), axis=0, keepdims=True)
        att_grad = dot_nt(branch, outw_ref[...])
        scaled = att_grad / tot_ref[...]
        weigh = scaled * att_ref[...]
        feature = lax.broadcasted_iota(jnp.int32, (width, LANES), 0) // HALF
        lane = lax.broadcasted_iota(jnp.int32, (width, LANES), 1)
        pick = (lane == 4 * feature).astype(F32).astype(BF16)
        high = weigh.astype(BF16)
        rest = (weigh - high.astype(F32)).astype(BF16)
        offset = dot(high, pick) + dot(rest, pick)
        first = offset.astype(BF16).astype(F32)
        offset = first + pltpu.roll(offset - first, 1, 1)
        offsets = offset[:span] + pltpu.roll(offset[span:], 2, 1)

        def store(head, piece):
            own_ref[:, head * LANES : (head + 1) * LANES] = piece.astype(BF16)

        pair_rows(scaled[:span], scaled[span:], store)
        part = 2 * width // groups
        each = heads // groups
        for turn in range(groups):
            owner = lax.rem(meta_ref[0] + turn, groups)
            share_ref[turn, :, :part] = own_ref[:, pl.ds(pl.multiple_of(owner * part, LANES), part)]
            share_ref[turn, :, part:] = pltpu.roll(
                offsets, lax.rem(LANES - 4 * each * owner, LANES), 1
            ).astype(BF16)


def value_part_kernel(heads, segs, count, meta_ref, grads_ref, et_hbm, send_ref, keep_ref, et_ref, masked_ref, part_ref, acc_ref, sem):
    span = grads_ref.shape[0]
    rows = 2
    here = meta_ref[rows * segs]
    copy = pltpu.make_async_copy(et_hbm, et_ref, sem)
    copy.start()
    acc_ref[...] = jnp.zeros_like(acc_ref)
    places = here * span + lax.broadcasted_iota(jnp.int32, grads_ref.shape, 0)
    side = lax.rem(lax.broadcasted_iota(jnp.int32, grads_ref.shape, 1), LANES) // HALF
    total_keys = count * span
    copy.wait()

    def one(turn, carry):
        row, index = turn // segs, lax.rem(turn, segs)
        start, length = segment_bounds(meta_ref, row * segs, index, segs)
        end = start + length

        @pl.when((start < (here + 1) * span) & (end > here * span))
        def _():
            inside = (places >= start) & (places < end) & (side == row)
            masked_ref[...] = jnp.where(inside, grads_ref[...].astype(F32), 0.0).astype(BF16)

            def chunk(at, state):
                for head in range(heads):
                    part_ref[
                        pl.ds(pl.multiple_of(at * CHUNK, CHUNK), CHUNK),
                        head * LANES : (head + 1) * LANES,
                    ] = dot(
                        et_ref[at, head], masked_ref[:, head * LANES : (head + 1) * LANES]
                    ).astype(BF16)
                return state

            chunks = (length + CHUNK - 1) // CHUNK
            lax.fori_loop(0, chunks, chunk, 0)
            limit = jnp.maximum(chunks * CHUNK - 2 * LANES, 0)

            def tile(at, state):
                first = at * LANES - start
                window = jnp.clip(((first + total_keys) // LANES) * LANES - total_keys, 0, limit)
                window = pl.multiple_of(window, LANES)
                row_at = lax.broadcasted_iota(jnp.int32, (LANES, 2 * LANES), 0) + first
                column = lax.broadcasted_iota(jnp.int32, (LANES, 2 * LANES), 1) + window
                hit = (row_at == column) & (row_at >= 0) & (row_at < length)
                acc_ref[at] += dot(
                    hit.astype(F32).astype(BF16), part_ref[pl.ds(window, 2 * LANES), :]
                ).astype(BF16)
                return state

            lax.fori_loop(start // LANES, (end + LANES - 1) // LANES, tile, 0)

        return carry

    lax.fori_loop(0, rows * segs, one, 0)
    for at in range(count // 2):
        keep_ref[at] = acc_ref[here ^ (2 * at)]
        send_ref[at] = acc_ref[here ^ (2 * at + 1)]


def logit_kernel(heads, segs, groups, meta_ref, e_ref, values_hbm, *rest):
    shares = rest[:groups]
    out_ref = rest[groups]
    values_ref, aug_ref, lhs_ref, acc_ref, stage_ref, sems = rest[groups + 1 :]
    span = shares[0].shape[0]
    rows = 2
    part = heads * LANES
    lens_count = groups * rows * segs
    here = meta_ref[lens_count]
    copies = [pltpu.make_async_copy(values_hbm, values_ref, sems.at[groups])]
    copies[0].start()
    for turn in range(groups):
        copy = pltpu.make_async_copy(shares[turn], stage_ref.at[turn], sems.at[turn])
        copy.start()
        copies.append(copy)
    acc_ref[...] = jnp.zeros_like(acc_ref)
    for copy in copies:
        copy.wait()
    places = here * span + lax.broadcasted_iota(jnp.int32, (span, LANES), 0)
    lane = lax.broadcasted_iota(jnp.int32, (span, LANES), 1)

    def one(turn, carry):
        source = turn // (rows * segs)
        row = lax.rem(turn // segs, rows)
        index = lax.rem(turn, segs)
        start, length = segment_bounds(meta_ref, (source * rows + row) * segs, index, segs)
        end = start + length

        @pl.when((start < (here + 1) * span) & (end > here * span))
        def _():
            inside = (places >= start) & (places < end)
            own = (lane // HALF) == row
            spot = lane - HALF * (1 - row)
            offsets = stage_ref[source, :, part:].astype(F32)
            for head in range(heads):
                shift = lax.rem(HALF * (1 - row) - 4 * head - 2 * row + 2 * LANES, LANES)
                moved = pltpu.roll(offsets, shift, 1)
                fill = jnp.where((spot == 0) | (spot == 1), -moved, 0.0)
                grad = stage_ref[source, :, head * LANES : (head + 1) * LANES].astype(F32)
                lhs_ref[head] = jnp.where(inside, jnp.where(own, grad, fill), 0.0).astype(BF16)

            def chunk(at, state):
                moved = shift_tile(
                    values_ref,
                    start + at * CHUNK,
                    pl.multiple_of(source * part, LANES),
                    part,
                    at * CHUNK,
                    length,
                )
                place = lax.rem(lax.broadcasted_iota(jnp.int32, moved.shape, 1), LANES)
                within = lax.broadcasted_iota(jnp.int32, moved.shape, 0) + at * CHUNK < length
                aug_ref[...] = jnp.where((place // HALF) == row, moved, within.astype(F32)).astype(
                    BF16
                )
                for head in range(heads):
                    acc_ref[at, head] += dot_nt(
                        lhs_ref[head], aug_ref[:, head * LANES : (head + 1) * LANES]
                    )
                return state

            lax.fori_loop(0, (length + CHUNK - 1) // CHUNK, chunk, 0)

        return carry

    lax.fori_loop(0, groups * rows * segs, one, 0)
    out_ref[...] = (acc_ref[...] * e_ref[...].astype(F32)).astype(BF16)


def spread_kernel(meta_ref, piece_ref, *rest):
    out_ref = rest[-1]
    chunks = piece_ref.shape[0]
    for at in range(chunks):
        out_ref[:, :, at * CHUNK : (at + 1) * CHUNK] = piece_ref[at].astype(F32)


def cut_rows(full_ref, index, size):
    return full_ref[pl.ds(pl.multiple_of(index * size, 16), size), :].astype(BF16)


def weight_grad_kernel(count, narrow, meta_ref, left_ref, right_ref, *rest):
    extra = rest[:2] if narrow else ()
    send_ref, keep_ref = rest[len(extra) : len(extra) + 2]
    scratch = rest[len(extra) + 2 :]
    step = pl.program_id(0)
    half = count // 2
    size = send_ref.shape[1] - narrow

    if narrow:

        @pl.when(step == 0)
        def _():
            scratch[0][...] = dot_tn(extra[0][...], extra[1][...])

    main = dot_tn(left_ref[...], right_ref[...]).astype(BF16)
    for target, first, odd in ((send_ref, 0, 1), (keep_ref, half, 0)):

        @pl.when((step >= first) & (step < first + half))
        def _():
            target[0, :size] = main
            if narrow:
                member = meta_ref[0] ^ (2 * (step - first) + odd)
                target[0, size:] = cut_rows(scratch[0], member, narrow)


def weight_grad_whole_kernel(count, narrow, meta_ref, left_ref, right_ref, *rest):
    extra = rest[:2] if narrow else ()
    send_ref, keep_ref = rest[len(extra) : len(extra) + 2]
    scratch = rest[len(extra) + 2 :]
    size = send_ref.shape[1] - narrow
    scratch[-1][...] = dot_tn(left_ref[...], right_ref[...])
    if narrow:
        scratch[0][...] = dot_tn(extra[0][...], extra[1][...])
    for at in range(count // 2):
        for target, odd in ((send_ref, 1), (keep_ref, 0)):
            member = meta_ref[0] ^ (2 * at + odd)
            target[at, :size] = cut_rows(scratch[-1], member, size)
            if narrow:
                target[at, size:] = cut_rows(scratch[0], member, narrow)


def tail_kernel(
    heads,
    count,
    meta_ref,
    low_ref,
    high_ref,
    x_ref,
    first_ref,
    h1_grad_ref,
    gain_ref,
    weight_ref,
    small2_ref,
    upb_grad_ref,
    input_grad_ref,
    send_ref,
    keep_ref,
    tok_ref,
    full_ref,
    small_ref,
):
    rows, span, width = x_ref.shape
    half = heads // 2

    def load(head):
        source = low_ref if head < half else high_ref
        at = head % half
        return source[:, at * LANES : (at + 1) * LANES].astype(F32)

    def store(row, at, piece):
        tok_ref[row * span : (row + 1) * span, at * LANES : (at + 1) * LANES] = piece.astype(BF16)

    unpair_rows(load, heads, store)
    grads = tok_ref[...]
    full_ref[...] = dot_tn(first_ref[...], grads)
    back = dot_nt(grads, weight_ref[...])
    xhat, inverse = standardize(x_ref[...].reshape(rows * span, width).astype(F32))
    input_grad_ref[...] = (
        h1_grad_ref[...] + norm_backward(back * gain_ref[...], xhat, inverse)
    ).reshape(rows, span, width)
    small_ref[...] = jnp.zeros_like(small_ref)
    small_ref[0:1] = jnp.sum(back * xhat, axis=0, keepdims=True)
    small_ref[1:2] = jnp.sum(back, axis=0, keepdims=True)
    small_ref[2:6] = small2_ref[0:4]
    for at in range(upb_grad_ref.shape[1] // width):
        small_ref[6 + at : 7 + at] = upb_grad_ref[:, at * width : (at + 1) * width]
    small = small_ref[...].astype(BF16)
    size = keep_ref.shape[1] - small.shape[0]
    for at in range(count // 2):
        for target, odd in ((send_ref, 1), (keep_ref, 0)):
            target[at, :size] = cut_rows(full_ref, meta_ref[0] ^ (2 * at + odd), size)
            target[at, size:] = small


def finish_kernel(groups, plan, *refs):
    meta_ref = refs[0]
    pieces = refs[1:-len(plan)]
    outs = refs[-len(plan):]
    outer = (meta_ref[0] == 0) | (meta_ref[0] == groups - 1)
    parts = []
    for at in range(0, len(pieces), 2):
        middle, outward = pieces[at][...].astype(F32), pieces[at + 1][...].astype(F32)
        parts.append(jnp.where(outer, outward, middle))
    joined = jnp.concatenate(parts, axis=0)
    begin = 0
    for (size, turned), out_ref in zip(plan, outs):
        piece = joined[begin : begin + size]
        out_ref[...] = piece.T if turned else piece
        begin += size


def swap(piece, distance, count):
    return lax.ppermute(piece, "seq", [(at, at ^ distance) for at in range(count)])


def gather_blocks(low, high, count):
    bits = [1 << at for at in range(1, count.bit_length() - 1)]
    low_held, high_held = {0: low}, {0: high}
    for low_bit, high_bit in zip(bits, bits[::-1]):
        for held, bit in ((low_held, low_bit), (high_held, high_bit)):
            for offset, piece in list(held.items()):
                held[offset ^ bit] = swap(piece, bit, count)
    for held in (low_held, high_held):
        for offset, piece in list(held.items()):
            held[offset ^ 1] = swap(piece, 1, count)
    order = list(range(count))
    flat = []
    for offset in order:
        flat += [low_held[offset], high_held[offset]]
    return (order, flat)


def add(left, right):
    return (left.astype(F32) + right.astype(F32)).astype(BF16)


def scatter_sum(send, keep, count, axis):
    total = add(keep, swap(send, 1, count))
    size = total.shape[axis] // 2
    halves = [
        lax.slice_in_dim(total, 0, size, axis=axis),
        lax.slice_in_dim(total, size, 2 * size, axis=axis),
    ]
    bits = list(range(count.bit_length() - 2))
    for low_bit, high_bit in zip(bits, bits[::-1]):
        for side, bit in ((0, low_bit), (1, high_bit)):
            piece = halves[side]
            members = [m for m in range(count // 2) if not any((m >> b) & 1 for b in (bits[: bits.index(bit)] if side == 0 else bits[bits.index(bit) + 1 :]))]
            stay = [at for at, m in enumerate(members) if not (m >> bit) & 1]
            leave = [at for at, m in enumerate(members) if (m >> bit) & 1]
            going = jnp.stack([piece[at] for at in leave])
            halves[side] = add(
                jnp.stack([piece[at] for at in stay]), swap(going, 2 << bit, count)
            )
    return [half[0] for half in halves]


def dp_sum(piece, groups):
    if groups != 4:
        total = lax.psum(piece, "dp")
        return (total, total)
    inward = add(piece, lax.ppermute(piece, "dp", [(0, 1), (3, 2)]))
    middle = add(inward, lax.ppermute(inward, "dp", [(1, 2), (2, 1)]))
    return (middle, lax.ppermute(middle, "dp", [(1, 0), (2, 3)]))


def ring(piece, turn, groups):
    return lax.ppermute(piece, "dp", [(at, (at + turn) % groups) for at in range(groups)])


def local(
    inputs,
    lengths,
    ln1_gain,
    ln1_bias,
    value_weight,
    out_weight,
    out_bias,
    ln2_gain,
    ln2_bias,
    up_weight,
    up_bias,
    down_weight,
    down_bias,
    logit_table,
    cotangent,
):
    rows, span, width = inputs.shape
    heads, unused_span, full = logit_table.shape
    segs = lengths.shape[1]
    hidden_units = up_weight.shape[1]
    tokens = rows * span
    count = lax.axis_size("seq")
    groups = lax.axis_size("dp")
    here = lax.axis_index("seq").astype(jnp.int32)
    group = lax.axis_index("dp").astype(jnp.int32)
    chunks = full // CHUNK
    split = heads % groups == 0
    parts = groups if split else 1
    each = heads // parts
    group_at = group if split else jnp.int32(0)

    def sds(shape, dtype):
        return jax.ShapeDtypeStruct(shape, dtype)

    group_meta = group_at.reshape(1)
    here_meta = here.reshape(1)
    own_meta = jnp.concatenate([lengths.reshape(-1), here_meta])
    all_lengths = [lengths] + [ring(lengths, t, groups) for t in range(1, parts)]
    all_lengths = jnp.concatenate([piece.reshape(-1) for piece in all_lengths])
    all_meta = jnp.concatenate([all_lengths, here_meta])

    first, values_low, values_high, value_shares = pl.pallas_call(
        lambda *refs: prep_kernel(parts, *refs),
        out_shape=(
            sds((tokens, width), BF16),
            sds((span, width), BF16),
            sds((span, width), BF16),
            sds((parts, span, 2 * width // parts), BF16),
        ),
        in_specs=[smem()] + [whole()] * 4,
        out_specs=[whole()] * 4,
        scratch_shapes=[pltpu.VMEM((span, 2 * width), BF16)],
        compiler_params=params(32),
        cost_estimate=cost(2 * tokens * width * width, 3e6),
        name="prep",
    )(group_meta, inputs, ln1_gain, ln1_bias, value_weight)

    order, blocks = gather_blocks(values_low, values_high, count)

    weights, weights_t = pl.pallas_call(
        exp_kernel,
        grid=(heads,),
        out_shape=(
            sds((chunks, heads, span, CHUNK), BF16),
            sds((chunks, heads, CHUNK, span), BF16),
        ),
        in_specs=[pl.BlockSpec((1, span, full), lambda h: (h, 0, 0))],
        out_specs=[
            pl.BlockSpec((chunks, 1, span, CHUNK), lambda h: (0, h, 0, 0)),
            pl.BlockSpec((chunks, 1, CHUNK, span), lambda h: (0, h, 0, 0)),
        ],
        compiler_params=params(32),
        cost_estimate=cost(4e9, 1e7),
        name="table_exp",
    )(logit_table)

    if split:
        pieces = [value_shares[0]] + [ring(value_shares[t], t, groups) for t in range(1, groups)]
    else:
        pieces = [values_low, values_high]
    other_values = lax.all_gather(jnp.concatenate(pieces, axis=1), "seq", axis=0, tiled=True)

    att_low, attended, totals, hidden1, second = pl.pallas_call(
        lambda *refs: attend_kernel(heads, segs, order, *refs),
        out_shape=(
            sds((tokens, width), BF16),
            sds((tokens, width), F32),
            sds((tokens, width), F32),
            sds((tokens, width), F32),
            sds((tokens, width), BF16),
        ),
        in_specs=[smem()] + [whole()] * 5 + [anywhere()] * (1 + 2 * count),
        out_specs=[whole()] * 5,
        scratch_shapes=[
            pltpu.VMEM((chunks, heads, span, CHUNK), BF16),
            pltpu.VMEM((full, 2 * width), BF16),
            pltpu.VMEM((CHUNK, 2 * width), BF16),
            pltpu.VMEM((heads, span, LANES), F32),
            pltpu.VMEM((rows, heads, span, LANES), F32),
            pltpu.SemaphoreType.DMA((2 * count + 1,)),
        ],
        compiler_params=params(48),
        cost_estimate=cost(6e9, 1e7),
        name="attend",
    )(
        own_meta,
        inputs,
        out_weight,
        out_bias,
        ln2_gain,
        ln2_bias,
        weights,
        *blocks,
    )

    step = math.gcd(hidden_units, 512)
    steps = hidden_units // step
    part = 2 * width // parts

    def full_block(shape):
        return pl.BlockSpec(shape, lambda i: (0,) * len(shape))

    (
        layer_out,
        act,
        pre_grad,
        up_bias_part,
        hidden1_grad,
        branch,
        grad_shares,
        own_grads,
        small2,
    ) = pl.pallas_call(
        lambda *refs: ffn_kernel(heads, parts, span, *refs),
        grid=(steps,),
        out_shape=(
            sds((tokens, width), BF16),
            sds((tokens, hidden_units), BF16),
            sds((tokens, hidden_units), BF16),
            sds((1, hidden_units), F32),
            sds((tokens, width), F32),
            sds((tokens, width), BF16),
            sds((parts, span, part + LANES), BF16),
            sds((span, 2 * width), BF16),
            sds((8, width), F32),
        ),
        in_specs=[
            smem(),
            full_block((tokens, width)),
            full_block((tokens, width)),
            full_block((tokens, width)),
            pl.BlockSpec((width, step), lambda i: (0, i)),
            pl.BlockSpec((step,), lambda i: (i,)),
            pl.BlockSpec((step, width), lambda i: (i, 0)),
            full_block((width,)),
            full_block((width, width)),
            full_block((width,)),
            full_block((tokens, width)),
            full_block((tokens, width)),
        ],
        out_specs=[
            full_block((tokens, width)),
            pl.BlockSpec((tokens, step), lambda i: (0, i)),
            pl.BlockSpec((tokens, step), lambda i: (0, i)),
            pl.BlockSpec((1, step), lambda i: (0, i)),
            full_block((tokens, width)),
            full_block((tokens, width)),
            full_block((parts, span, part + LANES)),
            full_block((span, 2 * width)),
            full_block((8, width)),
        ],
        scratch_shapes=[pltpu.VMEM((tokens, width), F32), pltpu.VMEM((tokens, width), F32)],
        compiler_params=params(48, ("arbitrary",)),
        cost_estimate=cost(8 * tokens * width * hidden_units, 2e7),
        name="ffn",
    )(
        group_meta,
        second,
        hidden1,
        cotangent.reshape(tokens, width),
        up_weight,
        up_bias,
        down_weight,
        down_bias,
        out_weight,
        ln2_gain,
        attended,
        totals,
    )

    if split:
        shares = [grad_shares[0]] + [ring(grad_shares[t], t, groups) for t in range(1, groups)]
    else:
        shares = [grad_shares[0]]
    logit_part = pl.pallas_call(
        lambda *refs: logit_kernel(each, segs, parts, *refs),
        grid=(1,),
        out_shape=sds((chunks, each, span, CHUNK), BF16),
        in_specs=[
            smem(),
            pl.BlockSpec(
                (chunks, each, span, CHUNK),
                (lambda i: (0, lax.axis_index("dp"), 0, 0)) if split else (lambda i: (0, 0, 0, 0)),
            ),
        ]
        + [anywhere()] * (parts + 1),
        out_specs=full_block((chunks, each, span, CHUNK)),
        scratch_shapes=[
            pltpu.VMEM((full, 2 * width), BF16),
            pltpu.VMEM((CHUNK, each * LANES), BF16),
            pltpu.VMEM((each, span, LANES), BF16),
            pltpu.VMEM((chunks, each, span, CHUNK), F32),
            pltpu.VMEM((parts, span, part + LANES), BF16),
            pltpu.SemaphoreType.DMA((parts + 1,)),
        ],
        compiler_params=params(48),
        cost_estimate=cost(8e9, 8e6),
        name="logit_grad",
    )(all_meta, weights, other_values, *shares)

    part_send, part_keep = pl.pallas_call(
        lambda *refs: value_part_kernel(heads, segs, count, *refs),
        out_shape=(
            sds((count // 2, span, 2 * width), BF16),
            sds((count // 2, span, 2 * width), BF16),
        ),
        in_specs=[smem(), whole(), anywhere()],
        out_specs=[whole()] * 2,
        scratch_shapes=[
            pltpu.VMEM((chunks, heads, CHUNK, span), BF16),
            pltpu.VMEM((span, 2 * width), BF16),
            pltpu.VMEM((full, 2 * width), BF16),
            pltpu.VMEM((count, span, 2 * width), BF16),
            pltpu.SemaphoreType.DMA(()),
        ],
        compiler_params=params(48),
        cost_estimate=cost(6e9, 1e7),
        name="value_part",
    )(own_meta, own_grads, weights_t)
    grads_low, grads_high = scatter_sum(part_send, part_keep, count, 2)

    def weight_grads(left, right, extra, narrow):
        size = left.shape[1] // count
        shape = (count // 2, size + narrow, width)
        scratch = [pltpu.VMEM((count * narrow, width), F32)] if narrow else []
        if size % LANES == 0:
            half = count // 2

            def member(i, meta):
                return (0, meta[0] ^ (2 * lax.rem(i, half) + jnp.where(i < half, 1, 0)))

            block = (1,) + shape[1:]
            return pl.pallas_call(
                lambda *refs: weight_grad_kernel(count, narrow, *refs),
                grid_spec=pltpu.PrefetchScalarGridSpec(
                    num_scalar_prefetch=1,
                    grid=(count,),
                    in_specs=[pl.BlockSpec((tokens, size), member)]
                    + [
                        pl.BlockSpec(piece.shape, lambda i, meta: (0, 0))
                        for piece in (right,) + extra
                    ],
                    out_specs=[
                        pl.BlockSpec(block, lambda i, meta: (jnp.minimum(i, half - 1), 0, 0)),
                        pl.BlockSpec(block, lambda i, meta: (jnp.maximum(i - half, 0), 0, 0)),
                    ],
                    scratch_shapes=scratch,
                ),
                out_shape=(sds(shape, BF16), sds(shape, BF16)),
                compiler_params=params(32, ("arbitrary",)),
                cost_estimate=cost(2 * tokens * width * hidden_units, 8e6),
                name="weight_grad",
            )(here_meta, left, right, *extra)
        return pl.pallas_call(
            lambda *refs: weight_grad_whole_kernel(count, narrow, *refs),
            out_shape=(sds(shape, BF16), sds(shape, BF16)),
            in_specs=[smem()] + [whole()] * (2 + len(extra)),
            out_specs=[whole()] * 2,
            scratch_shapes=scratch + [pltpu.VMEM((left.shape[1], width), F32)],
            compiler_params=params(48),
            cost_estimate=cost(2 * tokens * width * hidden_units, 8e6),
            name="weight_grad",
        )(here_meta, left, right, *extra)

    upstream = cotangent.reshape(tokens, width)
    narrow = width // count
    size = hidden_units // count
    down_halves = scatter_sum(
        *weight_grads(act, upstream, (att_low, branch), narrow), count, 1
    )
    up_halves = scatter_sum(*weight_grads(pre_grad, second, (), 0), count, 1)

    extra_rows = narrow + EXTRA
    input_grad, value_send, value_keep = pl.pallas_call(
        lambda *refs: tail_kernel(heads, count, *refs),
        out_shape=(
            sds((rows, span, width), F32),
            sds((count // 2, extra_rows, width), BF16),
            sds((count // 2, extra_rows, width), BF16),
        ),
        in_specs=[smem()] + [whole()] * 9,
        out_specs=[whole()] * 3,
        scratch_shapes=[
            pltpu.VMEM((tokens, width), BF16),
            pltpu.VMEM((width, width), F32),
            pltpu.VMEM((EXTRA, width), F32),
        ],
        compiler_params=params(32),
        cost_estimate=cost(4 * tokens * width * width, 6e6),
        name="tail",
    )(
        here_meta,
        grads_low,
        grads_high,
        inputs,
        first,
        hidden1_grad,
        ln1_gain,
        value_weight,
        small2,
        up_bias_part,
    )
    value_halves = scatter_sum(value_send, value_keep, count, 1)

    def finish(pieces, plan):
        flat = [piece for half in pieces for piece in dp_sum(half, groups)]
        return pl.pallas_call(
            lambda *refs: finish_kernel(groups, plan, *refs),
            out_shape=tuple(
                sds((width, rows_out) if turned else (rows_out, width), F32)
                for rows_out, turned in plan
            ),
            in_specs=[smem()] + [whole()] * len(flat),
            out_specs=[whole()] * len(plan),
            compiler_params=params(32),
            cost_estimate=cost(1e6, 4e6),
            name="finish",
        )(group.reshape(1), *flat)

    down_weight_grad, out_weight_grad = finish(down_halves, ((size, False), (narrow, False)))
    (up_weight_grad,) = finish(up_halves, ((size, True),))
    value_weight_grad, small = finish(
        [jnp.concatenate(value_halves, axis=0)], ((narrow, False), (EXTRA, False))
    )

    def mine(vector):
        length = vector.shape[0] // count
        return lax.dynamic_slice_in_dim(vector, here * length, length, 0)

    def spread(piece, turn, target):
        return pl.pallas_call(
            spread_kernel,
            grid_spec=pltpu.PrefetchScalarGridSpec(
                num_scalar_prefetch=1,
                grid=(each,),
                in_specs=[pl.BlockSpec((chunks, 1, span, CHUNK), lambda h, meta: (0, h, 0, 0))]
                + [anywhere()] * len(target),
                out_specs=pl.BlockSpec(
                    (1, span, full),
                    lambda h, meta: (lax.rem(meta[0] + parts - turn, parts) * each + h, 0, 0),
                ),
            ),
            out_shape=sds((heads, span, full), F32),
            input_output_aliases={2: 0} if target else {},
            compiler_params=params(32, ("arbitrary",)),
            cost_estimate=cost(1e6, 5e6),
            name="spread",
        )(group_meta, piece, *target)

    if split:
        piece = logit_part
        logit_grad = spread(piece, 0, ())
        for turn in range(1, groups):
            piece = ring(piece, 1, groups)
            logit_grad = spread(piece, turn, (logit_grad,))
    else:
        summed = lax.psum(logit_part, "dp").astype(F32)
        logit_grad = jnp.transpose(summed, (1, 2, 0, 3)).reshape(heads, span, full)

    return (
        layer_out.reshape(rows, span, width),
        input_grad,
        mine(small[0]),
        mine(small[1]),
        value_weight_grad,
        out_weight_grad,
        mine(small[5]),
        mine(small[3]),
        mine(small[4]),
        up_weight_grad,
        mine(small[6 : 6 + hidden_units // width].reshape(hidden_units)),
        down_weight_grad,
        mine(small[2]),
        logit_grad,
    )


def solution(mesh):
    return jax.shard_map(
        local,
        mesh=mesh,
        in_specs=(
            P("dp", "seq", None),
            P("dp", None),
            P(),
            P(),
            P(),
            P(),
            P(),
            P(),
            P(),
            P(),
            P(),
            P(),
            P(),
            P(None, "seq", None),
            P("dp", "seq", None),
        ),
        out_specs=(
            P("dp", "seq", None),
            P("dp", "seq", None),
            P("seq"),
            P("seq"),
            P("seq", None),
            P("seq", None),
            P("seq"),
            P("seq"),
            P("seq"),
            P(None, "seq"),
            P("seq"),
            P("seq", None),
            P("seq"),
            P(None, "seq", None),
        ),
        check_vma=False,
    )
```

```python
import math

import jax
import jax.numpy as jnp
from jax import lax
from jax.experimental import pallas as pl
from jax.experimental.pallas import tpu as pltpu
from jax.sharding import PartitionSpec as P

EPSILON = 1e-05
CHUNK = 256
WINDOW = 384
LANES = 128
HALF = 64
GELU_SCALE = math.sqrt(2.0 / math.pi)
GELU_CUBE = 0.044715
F32 = jnp.float32
BF16 = jnp.bfloat16


EXPECTED = {
    "prep": 30,
    "table_exp": 30,
    "core": 200,
    "down_grad": 30,
    "up_value": 100,
    "logit": 160,
    "tail": 3.3,
    "layer": 20,
    "spread": 1.2,
    "space": 20,
    "long_space": 100,
}


def expected(name):
    micros = EXPECTED.get(name, 0.6)
    return pl.CostEstimate(flops=int(micros * 1.15e9), bytes_accessed=1000, transcendentals=0)


def sds(shape, dtype):
    return jax.ShapeDtypeStruct(tuple(shape), dtype)


def dot(left, right):
    return jnp.dot(left, right, preferred_element_type=F32)


def dot_nt(left, right):
    return lax.dot_general(left, right, (((1,), (1,)), ((), ())), preferred_element_type=F32)


def dot_tn(left, right):
    return lax.dot_general(left, right, (((0,), (0,)), ((), ())), preferred_element_type=F32)


def iota(shape, axis):
    return lax.broadcasted_iota(jnp.int32, shape, axis)


def standardize(values_in):
    center = values_in - jnp.mean(values_in, axis=-1, keepdims=True)
    inverse = lax.rsqrt(jnp.mean(center * center, axis=-1, keepdims=True) + EPSILON)
    return (center * inverse, inverse)


def norm_backward(upstream, normed, inverse):
    return inverse * (
        upstream
        - jnp.mean(upstream, axis=-1, keepdims=True)
        - normed * jnp.mean(upstream * normed, axis=-1, keepdims=True)
    )


class Fast:
    def __init__(self, array):
        self.array = array


GRANTS = {
    "prep": 58,
    "table_exp": 58,
    "core": 54,
    "down_grad": 16,
    "up_value": 30,
    "logit": 58,
}


def grant(name, scratch):
    need = 6 * 1024 * 1024
    for piece in scratch:
        if piece.memory_space == pltpu.VMEM:
            need += math.prod(piece.shape) * jnp.dtype(piece.dtype).itemsize * 5 // 4
    least = GRANTS.get(name, 10) * 1024 * 1024
    return pltpu.CompilerParams(vmem_limit_bytes=min(max(least, need), 60 * 1024 * 1024))


class Chain:
    def __init__(self):
        self.token = None

    def space(self, name="space"):
        self.run(name, lambda *unused: None, [], [])

    def run(self, name, body, ins, outs, scratch=(), meta=None, copies=32, chained=True, aliases=None):
        fast_in = [isinstance(piece, Fast) for piece in ins]
        fast_out = [isinstance(piece, Fast) for piece in outs]
        ins = [piece.array if isinstance(piece, Fast) else piece for piece in ins]
        outs = [piece.array if isinstance(piece, Fast) else piece for piece in outs]
        token = [] if self.token is None or not chained else [self.token]
        spaces = {True: pltpu.VMEM, False: pltpu.HBM}
        n_meta, n_in, n_out = int(meta is not None), len(ins), len(outs)

        def kernel(*refs):
            refs = list(refs)
            meta_ref = refs.pop(0) if n_meta else None
            in_refs = refs[:n_in]
            del refs[: n_in + len(token)]
            out_refs = refs[:n_out]
            del refs[: n_out + 1]
            sems = refs.pop()
            used = []

            def move(source, target):
                copy = pltpu.make_async_copy(source, target, sems.at[len(used)])
                used.append(copy)
                copy.start()
                return copy

            body(meta_ref, in_refs, out_refs, refs, move)

        results = pl.pallas_call(
            kernel,
            out_shape=tuple(outs) + (sds((8, LANES), F32),),
            in_specs=[pl.BlockSpec(memory_space=pltpu.SMEM)] * n_meta
            + [pl.BlockSpec(memory_space=spaces[fast]) for fast in fast_in]
            + [pl.BlockSpec(memory_space=pl.ANY)] * len(token),
            out_specs=[pl.BlockSpec(memory_space=spaces[fast]) for fast in fast_out]
            + [pl.BlockSpec(memory_space=pl.ANY)],
            scratch_shapes=list(scratch) + [pltpu.SemaphoreType.DMA((copies,))],
            input_output_aliases={n_meta + at: to for at, to in (aliases or {}).items()},
            compiler_params=grant(name, scratch),
            cost_estimate=expected(name),
            name=name,
        )(*([meta] if n_meta else []), *ins, *token)
        if chained:
            self.token = results[-1]
        return results[:-1]


def vmem(shape, dtype):
    return pltpu.VMEM(tuple(shape), dtype)


def like(array, dtype=None):
    return pltpu.VMEM(tuple(array.shape), dtype or array.dtype)


def segment(lengths, index, segs):
    start = jnp.int32(0)
    for at in range(segs):
        start = start + jnp.where(at < index, lengths[at], 0)
    return (start, jnp.where(index < segs, lengths[jnp.minimum(index, segs - 1)], 0))


class RowLengths:
    def __init__(self, ref, row):
        self.ref, self.row = ref, row

    def __getitem__(self, index):
        return self.ref[self.row, index]


class Lengths:
    def __init__(self, ref, source, base):
        self.ref, self.source, self.base = ref, source, base

    def __getitem__(self, index):
        return self.ref[self.source, 0, HALF + 2 * (self.base + index)]


def first_segment(lengths, place, segs):
    index, end = jnp.int32(0), jnp.int32(0)
    for at in range(segs):
        end = end + lengths[at]
        index = index + jnp.where(end <= place, 1, 0)
    return index


def overlapped(lengths, index, begin, end, segs):
    start, length = segment(lengths, index, segs)
    touches = (start < end) & (start + length > begin)
    return (jnp.where(touches, start, 0), jnp.where(touches, length, 0))


def chunk_count(lengths):
    longest = lengths[0]
    for length in lengths[1:]:
        longest = jnp.maximum(longest, length)
    return (longest + CHUNK - 1) // CHUNK


def shifter(start):
    hit = iota((WINDOW, CHUNK), 0) == iota((WINDOW, CHUNK), 1) + lax.rem(start, LANES)
    return hit.astype(F32).astype(BF16)


def shifted(values_ref, rows, move_ref, start, length, at):
    window = jnp.minimum((start // LANES) * LANES + at * CHUNK, values_ref.shape[1] - WINDOW)
    window = pl.multiple_of(window, LANES)
    mover = jnp.where(iota((WINDOW, CHUNK), 1) < length - at * CHUNK, move_ref[...], 0)
    return dot(values_ref[rows, pl.ds(window, WINDOW)], mover)


def row_blocks(count):
    return [slice(at, at + 16) for at in range(0, count, 16)]


def put_shares(values, target, offsets, rows, groups):
    width = values.shape[0] // rows
    part = width // groups
    for at, offset in enumerate(offsets):
        owner = lax.axis_index("dp") ^ offset
        for row in range(rows):
            begin = pl.multiple_of(row * width + owner * part, HALF)
            spot = (at * rows + row) * part
            target[spot : spot + part] = values[pl.ds(begin, part)]


def prep_kernel(groups, meta, ins, outs, scratch, move):
    x_ref, gain_ref, bias_ref, weight_ref, first_ref = scratch
    loads = [move(*pair) for pair in zip(ins, scratch)]
    rows, span, width = x_ref.shape
    for load in loads[:3]:
        load.wait()
    xhat, unused = standardize(x_ref[...].reshape(rows * span, width).astype(F32))
    first_ref[...] = (xhat * gain_ref[...] + bias_ref[...]).astype(BF16)
    store = move(first_ref, outs[0])
    loads[3].wait()
    turned = dot(first_ref[...], weight_ref[...]).T.astype(BF16)
    values = outs[1]
    for row in range(rows):
        values[row * width : (row + 1) * width] = turned[:, row * span : (row + 1) * span]
    if groups > 1:
        put_shares(values, outs[2], (1, 3), rows, groups)
    store.wait()


def exp_kernel(groups, meta, ins, outs, scratch, move):
    table_ref, e_ref = scratch
    chunks, heads = e_ref.shape[:2]
    loads = [move(ins[0].at[head], table_ref.at[head]) for head in range(heads)]
    stores = []
    for head in range(heads):
        loads[head].wait()
        e = jnp.exp(table_ref[head].astype(F32)).astype(BF16)
        for at in range(chunks):
            e_ref[at, head] = e[:, at * CHUNK : (at + 1) * CHUNK]
        stores.append(move(e_ref.at[:, head], outs[0].at[:, head]))
    if groups > 1:
        values, got = ins[1:]
        half = got.shape[0] // 2
        put_shares(values, outs[1], (2,), 2, groups)
        outs[1][half:] = got[half:]
    for store in stores:
        store.wait()


def gather_kernel(groups, meta, ins, outs, scratch, move):
    near = ins[: len(outs) - 1]
    joined = outs[-1]
    if groups > 1:
        (own_ref,) = scratch
        first, second = ins[len(near) :]
        put_shares(ins[0], own_ref, (0,), 2, groups)
        size = own_ref.shape[0]
        copies = [
            move(own_ref, joined.at[pl.ds(0, size)]),
            move(first.at[pl.ds(0, size)], joined.at[pl.ds(size, size)]),
            move(second, joined.at[pl.ds(2 * size, 2 * size)]),
        ]
    else:
        copies = [move(ins[0], joined)]
    for source, target in zip(near, outs):
        target[...] = source[...]
    for copy in copies:
        copy.wait()


def share_kernel(meta, ins, outs, scratch, move):
    copies = [move(piece, outs[0].at[at]) for at, piece in enumerate(ins)]
    for copy in copies:
        copy.wait()


def core_kernel(heads, segs, groups, order, meta, ins, outs, scratch, move):
    (
        e_ref, x_ref, outw_ref, outb_ref, gain_ref, bias_ref, up_ref, upb_ref, g_ref, down_ref,
        values_ref, move_ref, aug_ref, acc_ref, res_ref, att_ref, tot_ref, h1_ref, back_ref, raw_ref,
        back_in_ref, h1_grad_ref, paired_ref, small_ref,
    ) = scratch
    low_ref, second_ref, act_ref, pre_ref, branch_ref, turned_out, act_out, h1_out, h1_grad_out, small_out = outs[:10]
    share_out = outs[10:]
    rows, span, width = x_ref.shape
    hidden_units = up_ref.shape[1]
    here = lax.axis_index("seq")
    blocks = ins[10:]
    loads = [move(*pair) for pair in zip(ins[:10], scratch[:10])]
    later = loads[1:]
    for at, offset in enumerate(order):
        place = pl.multiple_of((here ^ offset) * span, LANES)
        for row in range(rows):
            values_ref[row, :, pl.ds(place, span)] = blocks[at][row * width : (row + 1) * width]
    full = values_ref.shape[2] - CHUNK
    values_ref[:, :, full:] = jnp.zeros((rows, width, CHUNK), BF16)
    res_ref[...] = jnp.zeros_like(res_ref)
    begin, end = here * span, (here + 1) * span
    places = begin + iota((span, LANES), 0)
    lengths = [RowLengths(meta, row) for row in range(rows)]
    firsts = [first_segment(lengths[row], begin, segs) for row in range(rows)]
    loads[0].wait()

    def slot(turn, carry):
        bounds = [
            overlapped(lengths[row], firsts[row] + turn, begin, end, segs) for row in range(rows)
        ]
        count = chunk_count([length for unused, length in bounds])

        @pl.when(count > 0)
        def _():
            acc_ref[...] = jnp.zeros_like(acc_ref)
            for row, (start, unused) in enumerate(bounds):
                move_ref[row] = shifter(start)

            def chunk(at, state):
                for row, (start, length) in enumerate(bounds):
                    moved = shifted(
                        values_ref.at[row], slice(None), move_ref.at[row], start, length, at
                    ).astype(BF16)
                    ones = iota((HALF, CHUNK), 1) < length - at * CHUNK
                    ones = ones.astype(F32).astype(BF16)
                    for head in range(heads):
                        base = row * LANES
                        spots = (base, base + HALF) if head % 2 == 0 else (base + HALF, base)
                        aug_ref[head, spots[0] : spots[0] + HALF] = moved[head * HALF : (head + 1) * HALF]
                        aug_ref[head, spots[1] : spots[1] + HALF] = ones
                for head in range(heads):
                    acc_ref[head] += dot_nt(e_ref[at, head], aug_ref[head])
                return state

            lax.fori_loop(0, count, chunk, 0)
            for row, (start, length) in enumerate(bounds):
                inside = (places >= start) & (places < start + length)
                for head in range(heads):
                    res_ref[row, head] = jnp.where(
                        inside, acc_ref[head, :, row * LANES : (row + 1) * LANES], res_ref[row, head]
                    )

        return carry

    lax.fori_loop(0, segs, slot, 0)
    low_lanes = iota((span, LANES), 1) < HALF
    for row in range(rows):
        for pair in range(heads // 2):
            even, odd = res_ref[row, 2 * pair], res_ref[row, 2 * pair + 1]
            total = pltpu.roll(jnp.where(low_lanes, odd, even), HALF, 1)
            attended = jnp.where(low_lanes, even, odd) / total
            spot = (slice(row * span, (row + 1) * span), slice(pair * LANES, (pair + 1) * LANES))
            tot_ref[spot] = total
            att_ref[spot] = attended
            low_ref[spot] = attended.astype(BF16)
    stores = []
    for load in later:
        load.wait()
    tokens = rows * span
    blocks = row_blocks(tokens)
    h1_ref[...] = dot(low_ref[...], outw_ref[...])
    for spot in blocks:
        row, at = spot.start // span, spot.start % span
        hidden = h1_ref[spot] + x_ref[row, at : at + 16].astype(F32) + outb_ref[...]
        h1_ref[spot] = hidden
        xhat2, unused = standardize(hidden)
        second_ref[spot] = (xhat2 * gain_ref[...] + bias_ref[...]).astype(BF16)
    stores.append(move(h1_ref, h1_out))

    small_ref[...] = jnp.zeros_like(small_ref)
    g_low = g_ref[...].reshape(tokens, width)
    for index in range(hidden_units // width):
        cols = slice(index * width, (index + 1) * width)
        raw_ref[:, cols] = dot(second_ref[...], up_ref[:, cols])
        back_in_ref[:, cols] = dot_nt(g_low, down_ref[cols])
    half_width = width // 2
    for index in range(hidden_units // width):
        cols = slice(index * width, (index + 1) * width)
        for part in range(2):
            thin = slice(cols.start + part * half_width, cols.start + (part + 1) * half_width)
            upb = upb_ref[thin]
            tally = jnp.zeros((8, half_width), F32)
            for spot in blocks:
                pre = raw_ref[spot, thin] + upb
                square = pre * pre
                bent = jnp.tanh(pre * (GELU_SCALE + (GELU_SCALE * GELU_CUBE) * square))
                half = 0.5 + 0.5 * bent
                act_ref[spot, thin] = (pre * half).astype(BF16)
                slope = half + (pre * (half - half * bent)) * (
                    GELU_SCALE + (3.0 * GELU_SCALE * GELU_CUBE) * square
                )
                pre_grad = (back_in_ref[spot, thin] * slope).astype(BF16)
                pre_ref[spot, thin] = pre_grad
                wide = pre_grad.astype(F32)
                tally = tally + wide[:8] + wide[8:]
            small_ref[4 + index : 5 + index, part * half_width : (part + 1) * half_width] = jnp.sum(
                tally, axis=0, keepdims=True
            )
        stores.append(move(act_ref.at[:, cols], act_out.at[:, cols]))
        back = dot_nt(pre_ref[:, cols], up_ref[:, cols])
        back_ref[...] = back if index == 0 else back_ref[...] + back

    tallies = [jnp.zeros((8, width), F32)] * 4
    for spot in blocks:
        row, at = spot.start // span, spot.start % span
        back = back_ref[spot]
        wide = g_ref[row, at : at + 16].astype(F32)
        xhat2, inverse2 = standardize(h1_ref[spot])
        hidden_grad = wide + norm_backward(back * gain_ref[...], xhat2, inverse2)
        h1_grad_ref[spot] = hidden_grad
        branch = hidden_grad.astype(BF16)
        branch_ref[spot] = branch
        terms = (wide, back * xhat2, back, branch.astype(F32))
        tallies = [tally + term[:8] + term[8:] for tally, term in zip(tallies, terms)]
    for index, tally in enumerate(tallies):
        small_ref[index : index + 1] = jnp.sum(tally, axis=0, keepdims=True)
    stores.append(move(small_ref, small_out))
    stores.append(move(h1_grad_ref, h1_grad_out))
    att_grad = dot_nt(branch_ref[...], outw_ref[...])
    scaled = att_grad / tot_ref[...]
    weigh = scaled * att_ref[...]
    pick = (iota((width, LANES), 1) == 4 * (iota((width, LANES), 0) // HALF)).astype(F32).astype(BF16)
    high = weigh.astype(BF16)
    rest = (weigh - high.astype(F32)).astype(BF16)
    offset = dot(high, pick) + dot(rest, pick)
    rounded = offset.astype(BF16).astype(F32)
    offset = rounded + pltpu.roll(offset - rounded, 1, 1)
    offsets = offset[:span] + pltpu.roll(offset[span:], 2, 1)
    codes = jnp.zeros((span, LANES), F32)
    lane = iota((span, LANES), 1)
    for index in range(rows * segs):
        length = meta[index // segs, index % segs]
        codes = jnp.where(lane == HALF + 2 * index, (length // HALF).astype(F32), codes)
        codes = jnp.where(lane == HALF + 2 * index + 1, lax.rem(length, HALF).astype(F32), codes)
    scaled0, scaled1 = scaled[:span], scaled[span:]
    for pair in range(heads // 2):
        part0 = scaled0[:, pair * LANES : (pair + 1) * LANES]
        part1 = scaled1[:, pair * LANES : (pair + 1) * LANES]
        even = jnp.where(low_lanes, part0, pltpu.roll(part1, HALF, 1))
        odd = jnp.where(low_lanes, pltpu.roll(part0, HALF, 1), part1)
        paired_ref[:, 2 * pair * LANES : (2 * pair + 1) * LANES] = even.astype(BF16)
        paired_ref[:, (2 * pair + 1) * LANES : (2 * pair + 2) * LANES] = odd.astype(BF16)
    part = 2 * width // groups
    each = heads // groups
    group = lax.axis_index("dp") if groups > 1 else 0
    for turn in range(groups):
        owner = group ^ turn
        begin_lane = pl.multiple_of(owner * part, LANES)
        share_out[turn][:, :part] = paired_ref[:, pl.ds(begin_lane, part)]
        spin = lax.rem(LANES - 4 * each * owner, LANES)
        spun = pltpu.roll(offsets, spin, 1)
        share_out[turn][:, part:] = jnp.where(lane < HALF, spun, codes).astype(BF16)
    for row, piece in enumerate((scaled0, scaled1)):
        turned_out[row * width : (row + 1) * width] = piece.T.astype(BF16)
    for store in stores:
        store.wait()


def value_part_kernel(heads, segs, count, base, grads_ref, e_ref, lhs_ref, part_ref, acc_ref, send, keep, meta):
    rows = 2
    span = grads_ref.shape[1]
    width = grads_ref.shape[0] // rows
    here = lax.axis_index("seq")
    begin, end = here * span, (here + 1) * span
    acc_ref[...] = jnp.zeros_like(acc_ref)
    places = begin + iota((HALF, span), 1)
    lengths = [RowLengths(meta, row) for row in range(rows)]
    firsts = [first_segment(lengths[row], begin, segs) for row in range(rows)]

    def slot(turn, carry):
        bounds = [
            overlapped(lengths[row], firsts[row] + turn, begin, end, segs) for row in range(rows)
        ]
        chunks = chunk_count([length for unused, length in bounds])

        @pl.when(chunks > 0)
        def _():
            for row, (start, length) in enumerate(bounds):
                inside = (places >= start) & (places < start + length)
                for head in range(heads):
                    spot = row * width + head * HALF
                    piece = grads_ref[spot : spot + HALF].astype(F32)
                    lhs_ref[head, row * HALF : (row + 1) * HALF] = jnp.where(inside, piece, 0.0).astype(BF16)

            def chunk(at, state):
                cols = pl.ds(pl.multiple_of(at * CHUNK, CHUNK), CHUNK)
                for head in range(heads):
                    piece = dot(lhs_ref[head], e_ref[at, head]).astype(BF16)
                    for row in range(rows):
                        part_ref[row, head * HALF : (head + 1) * HALF, cols] = piece[
                            row * HALF : (row + 1) * HALF
                        ]
                return state

            lax.fori_loop(0, chunks, chunk, 0)
            limit = chunks * CHUNK - 2 * LANES
            for row, (start, length) in enumerate(bounds):

                def tile(at, state):
                    first = at * LANES - start
                    window = jnp.clip(((first + count * span) // LANES) * LANES - count * span, 0, limit)
                    window = pl.multiple_of(window, LANES)
                    column = iota((2 * LANES, LANES), 1) + first
                    hit = (iota((2 * LANES, LANES), 0) + window == column) & (column < length)
                    moved = dot(
                        part_ref[row, :, pl.ds(window, 2 * LANES)], hit.astype(F32).astype(BF16)
                    )
                    acc_ref[at, row * width : (row + 1) * width] += moved.astype(BF16)
                    return state

                last = jnp.where(length > 0, (start + length + LANES - 1) // LANES, 0)
                lax.fori_loop(start // LANES, last, tile, 0)

        return carry

    lax.fori_loop(0, segs, slot, 0)
    high = rows * span
    for at in range(count // 2):
        for odd, target in ((1, send), (0, keep)):
            for index in range(rows * width // high):
                target[at, base : base + high, index * span : (index + 1) * span] = acc_ref[
                    here ^ (2 * at + odd), index * high : (index + 1) * high
                ]


def logit_kernel(heads, segs, groups, count, meta, ins, outs, scratch, move):
    weights, values, shares = ins
    values_ref, move_ref, aug_ref, lhs_ref, acc_ref, e_ref, stage_all, codes_ref, lens_ref = scratch
    rows = 2
    span = shares.shape[1]
    half = heads * HALF
    part = heads * LANES
    here = lax.axis_index("seq")
    group = lax.axis_index("dp") if groups > 1 else 0
    share_load = move(shares, stage_all)
    e_load = move(weights.at[:, pl.ds(group * heads, heads)], e_ref)
    loads = [
        move(values.at[at], values_ref.at[:, at * span : (at + 1) * span]) for at in range(count)
    ]
    acc_ref[...] = jnp.zeros_like(acc_ref)
    values_ref[:, count * span :] = jnp.zeros((values_ref.shape[0], CHUNK), BF16)
    begin, end = here * span, (here + 1) * span
    places = begin + iota((span, LANES), 0)
    lane = iota((span, LANES), 1)
    share_load.wait()
    for source in range(groups):
        parts = stage_all[source, :16, part:].astype(F32)
        whole = HALF * parts + pltpu.roll(parts, LANES - 1, 1)
        codes_ref[source] = whole[:8].astype(jnp.int32)
    loads.append(move(codes_ref, lens_ref))
    for load in loads:
        load.wait()

    def slot(sources, turn, carry):
        all_bounds = []
        for source in sources:
            bounds = []
            for row in range(rows):
                lens = Lengths(lens_ref, source, row * segs)
                index = first_segment(lens, begin, segs) + turn
                bounds.append(overlapped(lens, index, begin, end, segs))
            all_bounds.append(bounds)
        chunks = chunk_count([length for bounds in all_bounds for unused, length in bounds])

        @pl.when(chunks > 0)
        def _():
            for number, (source, bounds) in enumerate(zip(sources, all_bounds)):
                offsets = stage_all[source, :, part:].astype(F32)
                for row, (start, length) in enumerate(bounds):
                    move_ref[number, row] = shifter(start)
                    inside = (places >= start) & (places < start + length)
                    for head in range(heads):
                        grad = stage_all[source, :, head * LANES : (head + 1) * LANES].astype(F32)
                        if row == 1:
                            grad = pltpu.roll(grad, HALF, 1)
                        fill = pltpu.roll(offsets, (HALF - 4 * head - 2 * row) % LANES, 1)
                        fill = jnp.where((lane == HALF) | (lane == HALF + 1), -fill, 0.0)
                        lhs = jnp.where(inside, jnp.where(lane < HALF, grad, fill), 0.0)
                        lhs_ref[number, head, :, row * LANES : (row + 1) * LANES] = lhs.astype(BF16)

            def chunk(at, state):
                for number, (source, bounds) in enumerate(zip(sources, all_bounds)):
                    for row, (start, length) in enumerate(bounds):
                        place = (source * rows + row) * half
                        moved = shifted(
                            values_ref,
                            slice(place, place + half),
                            move_ref.at[number, row],
                            start,
                            length,
                            at,
                        ).astype(BF16)
                        ones = iota((HALF, CHUNK), 1) < length - at * CHUNK
                        ones = ones.astype(F32).astype(BF16)
                        for head in range(heads):
                            base = row * LANES
                            aug_ref[number, head, base : base + HALF] = moved[head * HALF : (head + 1) * HALF]
                            aug_ref[number, head, base + HALF : base + LANES] = ones
                for head in range(heads):
                    total = acc_ref[at, head]
                    for number in range(len(sources)):
                        total = total + dot(lhs_ref[number, head], aug_ref[number, head])
                    acc_ref[at, head] = total
                return state

            lax.fori_loop(0, chunks, chunk, 0)

        return carry

    for first in range(0, groups, 2):
        sources = list(range(first, min(first + 2, groups)))
        lax.fori_loop(0, segs, lambda turn, carry: slot(sources, turn, carry), 0)
    e_load.wait()
    outs[0][...] = (acc_ref[...] * e_ref[...].astype(F32)).astype(BF16)


def spread_kernel(count, place_of, picks, meta, ins, outs, scratch, move):
    (out_ref,) = scratch
    member = lax.axis_index("dp") if place_of else 0
    place = place_of(member) if place_of else 0
    pieces = ins[:count]
    chunks, heads = pieces[0].shape[:2]
    for source, target in zip(pieces[len(pieces) - len(outs) + 1 :], outs[1:]):
        target[...] = source[...]
    outer = (member == 0) | (member == 3)
    stores = []
    for head in range(heads):
        for at in range(chunks):
            values = pieces[picks[0]][at, head]
            if picks[0] != picks[1]:
                values = jnp.where(outer, values, pieces[picks[1]][at, head])
            out_ref[head, :, at * CHUNK : (at + 1) * CHUNK] = values.astype(F32)
        stores.append(move(out_ref.at[head], outs[0].at[place * heads + head]))
    for store in stores:
        store.wait()


def cut_rows(full_ref, index, size):
    return full_ref[pl.ds(pl.multiple_of(index * size, 16), size), :].astype(BF16)


def cut_product(count, left_ref, right, send, keep, here):
    size = left_ref.shape[1] // count
    for at in range(count // 2):
        for odd, target in ((1, send), (0, keep)):
            member = here ^ (2 * at + odd)
            if size % LANES == 0:
                left = left_ref[:, pl.ds(pl.multiple_of(member * size, LANES), size)]
                target[at, :size] = dot_tn(left, right).astype(BF16)
                continue
            wide = -(-size // LANES) * LANES
            begin = jnp.minimum((member * size // LANES) * LANES, left_ref.shape[1] - wide)
            begin = pl.multiple_of(begin, LANES)
            product = dot_tn(left_ref[:, pl.ds(begin, wide)], right)
            apart = member * size - begin
            for choice in range(0, wide - size + 1, HALF):

                @pl.when(apart == choice)
                def _():
                    target[at, :size] = product[choice : choice + size].astype(BF16)


def down_grad_kernel(count, narrow, meta, ins, outs, scratch, move):
    act_ref, low_ref, branch_ref = ins[1:]
    g_ref, full_ref = scratch
    move(ins[0], g_ref).wait()
    send, keep = outs
    size, padded = act_ref.shape[1] // count, send.shape[1]
    here = lax.axis_index("seq")
    cut_product(count, act_ref, g_ref[...], send, keep, here)
    full_ref[...] = dot_tn(low_ref[...], branch_ref[...])
    for at in range(count // 2):
        for odd, target in ((1, send), (0, keep)):
            target[at, size : size + narrow] = cut_rows(full_ref, here ^ (2 * at + odd), narrow)
            if padded > size + narrow:
                target[at, size + narrow :] = jnp.zeros((padded - size - narrow, target.shape[2]), BF16)


def up_value_kernel(heads, segs, count, meta, ins, outs, scratch, move):
    pre_ref, second_ref, grads_ref = ins[1:]
    e_ref, lhs_ref, part_ref, acc_ref = scratch
    load = move(ins[0], e_ref)
    send, keep = outs
    size = pre_ref.shape[1] // count
    cut_product(count, pre_ref, second_ref[...], send, keep, lax.axis_index("seq"))
    load.wait()
    value_part_kernel(
        heads, segs, count, size, grads_ref, e_ref, lhs_ref, part_ref, acc_ref, send, keep, meta
    )


def layer_kernel(meta, ins, outs, scratch, move):
    act_ref, down_ref, h1_ref, bias_ref, out_ref = scratch
    loads = [move(*pair) for pair in zip(ins, scratch)]
    for load in loads:
        load.wait()
    out_ref[...] = (h1_ref[...] + dot(act_ref[...], down_ref[...]) + bias_ref[...]).astype(BF16)
    move(out_ref, outs[0]).wait()


def tail_kernel(heads, count, meta, ins, outs, scratch, move):
    (
        x_ref, first_ref, h1_grad_ref, gain_ref, weight_ref, small2_ref, grads_ref, full_ref, small_ref, back_ref,
    ) = scratch
    loads = [move(*pair) for pair in zip(ins[1:], scratch)]
    input_grad, send, keep = outs
    rows, span, width = x_ref.shape
    high = rows * span
    for index in range(rows * width // high):
        turned = ins[0][:, index * span : (index + 1) * span].astype(F32).T.astype(BF16)
        row, begin = index * high // width, index * high % width
        grads_ref[row * span : (row + 1) * span, begin : begin + high] = turned
    for load in loads:
        load.wait()
    grads = grads_ref[...]
    full_ref[...] = dot_tn(first_ref[...], grads)
    back = dot_nt(grads, weight_ref[...])
    xhat, inverse = standardize(x_ref[...].reshape(rows * span, width).astype(F32))
    small_ref[...] = jnp.zeros_like(small_ref)
    small_ref[0:1] = jnp.sum(back * xhat, axis=0, keepdims=True)
    small_ref[1:2] = jnp.sum(back, axis=0, keepdims=True)
    small_ref[2 : 2 + small2_ref.shape[0]] = small2_ref[...]
    small = small_ref[...].astype(BF16)
    size = send.shape[1] - small.shape[0]
    here = lax.axis_index("seq")
    for at in range(count // 2):
        for odd, target in ((1, send), (0, keep)):
            target[at, :size] = cut_rows(full_ref, here ^ (2 * at + odd), size)
            target[at, size:] = small
    back_ref[...] = (
        h1_grad_ref[...] + norm_backward(back * gain_ref[...], xhat, inverse)
    ).reshape(rows, span, width)
    move(back_ref, input_grad).wait()


def sum_kernel(jobs, meta, ins, outs, scratch, move):
    for (left, left_at), (right, right_at), routes in jobs:
        for begin, size, target, index, place in routes:
            rows = slice(begin, begin + size)
            left_spot = rows if left_at is None else (left_at, rows)
            right_spot = rows if right_at is None else (right_at, rows)
            total = ins[left][left_spot].astype(F32) + ins[right][right_spot].astype(F32)
            spot = slice(place or 0, (place or 0) + size)
            outs[target][spot if index is None else (index, spot)] = total.astype(BF16)


def finish_kernel(groups, plan, meta, ins, outs, scratch, move):
    middle_ref, outer_ref = ins
    member = lax.axis_index("dp")
    outer = (member == 0) | (member == groups - 1)
    stores = []
    begin = 0
    for number, (size, turned) in enumerate(plan):
        spot = slice(begin, begin + size)
        picked = jnp.where(outer, outer_ref[spot].astype(F32), middle_ref[spot].astype(F32))
        scratch[number][...] = picked.T if turned else picked
        stores.append(move(scratch[number], outs[number]))
        begin += size
    for store in stores:
        store.wait()


def swap(piece, distance, count):
    return lax.ppermute(piece, "seq", [(at, at ^ distance) for at in range(count)])


def beside(piece, distance):
    return lax.ppermute(piece, "dp", [(at, at ^ distance) for at in range(4)])


def add_pieces(chain, name, arrays, jobs, outs):
    return chain.run(
        name,
        lambda *args: sum_kernel(jobs, *args),
        [Fast(array) for array in arrays],
        [Fast(sds(shape, BF16)) for shape in outs],
    )


class Scatter:
    def __init__(self, chain, name, send, keep, count):
        self.chain, self.name, self.count = chain, name, count
        self.keep = keep
        self.bits = list(range(count.bit_length() - 2))
        self.level = 0
        self.got = [swap(send, 1, count)]

    def step(self, hold=False):
        members, rows, width = self.keep.shape if self.level == 0 else self.stay[0].shape
        if self.level == 0:
            half = rows // 2
            outs = [(members // 2, half, width)] * 4
            jobs = []
            for m in range(members):
                a_out = (0 if m & 1 else 1, m >> 1)
                top = m >= members // 2
                b_out = (2 if top else 3, m % (members // 2))
                jobs.append(
                    (
                        (0, m),
                        (1, m),
                        [
                            (0, half, a_out[0], a_out[1], None),
                            (half, half, b_out[0], b_out[1], None),
                        ],
                    )
                )
            results = add_pieces(
                self.chain,
                self.name + "_add0",
                [self.keep, self.got[0]],
                jobs,
                outs,
            )
        else:
            outs = [(members // 2, rows, width)] * 4
            jobs = []
            for side in range(2):
                for m in range(members):
                    if side == 0:
                        spot = (0 if m & 1 else 1, m >> 1)
                    else:
                        spot = (2 if m >= members // 2 else 3, m % (members // 2))
                    jobs.append(
                        (
                            (2 * side, m),
                            (2 * side + 1, m),
                            [(0, rows, spot[0], spot[1], None)],
                        )
                    )
            results = add_pieces(
                self.chain,
                self.name + "_add" + str(self.level),
                [self.stay[0], self.got[0], self.stay[1], self.got[1]],
                jobs,
                outs,
            )
        self.stay = [results[1], results[3]]
        self.going = [results[0], results[2]]
        if not hold:
            self.send()
        return self

    def release(self):
        self.going = gate(self.chain, self.name + "_gate", self.going)
        self.send()

    def send(self):
        self.got = [
            swap(self.going[0], 2 << self.bits[self.level], self.count),
            swap(self.going[1], 2 << self.bits[-1 - self.level], self.count),
        ]
        self.level += 1

    def last(self, cuts=None):
        unused, rows, width = self.stay[0].shape
        cuts = cuts or [2 * rows]
        begins = [sum(cuts[:at]) for at in range(len(cuts))]
        jobs = []
        for side in range(2):
            routes = []
            for number, (begin, size) in enumerate(zip(begins, cuts)):
                low = max(begin, side * rows)
                high = min(begin + size, (side + 1) * rows)
                if low < high:
                    routes.append((low - side * rows, high - low, number, None, low - begin))
            jobs.append(((2 * side, 0), (2 * side + 1, 0), routes))
        return add_pieces(
            self.chain,
            self.name + "_last",
            [self.stay[0], self.got[0], self.stay[1], self.got[1]],
            jobs,
            [(size, width) for size in cuts],
        )


class Across:
    def __init__(self, chain, name, piece, groups):
        self.chain, self.name, self.groups, self.level = chain, name, groups, 0
        self.piece = piece
        if groups == 4:
            self.got = lax.ppermute(piece, "dp", [(0, 1), (3, 2)])

    def step(self):
        if self.groups != 4:
            if self.level == 0:
                self.piece = lax.psum(self.piece, "dp")
                self.got = self.piece
        else:
            shape = self.piece.shape
            self.piece = add_pieces(
                self.chain,
                self.name + "_dp" + str(self.level),
                [self.piece, self.got],
                [((0, None), (1, None), [(0, shape[0], 0, None, None)])],
                [shape],
            )[0]
            pairs = [(1, 2), (2, 1)] if self.level == 0 else [(1, 0), (2, 3)]
            self.got = lax.ppermute(self.piece, "dp", pairs)
        self.level += 1
        return self

    def finish(self, plan):
        shape = self.piece.shape
        outs = [sds((shape[1], size) if turned else (size, shape[1]), F32) for size, turned in plan]
        return self.chain.run(
            self.name + "_finish",
            lambda *args: finish_kernel(self.groups, plan, *args),
            [Fast(self.piece), Fast(self.got)],
            outs,
            [vmem(out.shape, F32) for out in outs],
        )


def local(
    inputs,
    lengths,
    ln1_gain,
    ln1_bias,
    value_weight,
    out_weight,
    out_bias,
    ln2_gain,
    ln2_bias,
    up_weight,
    up_bias,
    down_weight,
    down_bias,
    logit_table,
    cotangent,
):
    rows, span, width = inputs.shape
    heads, unused_span, full = logit_table.shape
    segs = lengths.shape[1]
    hidden_units = up_weight.shape[1]
    tokens = rows * span
    count = lax.axis_size("seq")
    groups = lax.axis_size("dp")
    here = lax.axis_index("seq")
    chunks = full // CHUNK
    split = groups == 4 and heads % groups == 0
    parts = groups if split else 1
    each = heads // parts
    chain = Chain()

    part = width // parts
    passed = [Fast(sds((2 * rows * part, span), BF16))] * split
    first, own_values, *early = chain.run(
        "prep",
        lambda *args: prep_kernel(parts, *args),
        [inputs, ln1_gain, ln1_bias, value_weight],
        [sds((tokens, width), BF16), Fast(sds((rows * width, span), BF16))] + passed,
        [like(inputs), like(ln1_gain), like(ln1_bias), like(value_weight)]
        + [vmem((tokens, width), BF16)],
    )
    near = [swap(own_values, offset, count) for offset in range(2, count, 2)]
    early = [beside(piece, 1) for piece in early]
    weights, *later = chain.run(
        "table_exp",
        lambda *args: exp_kernel(parts, *args),
        [logit_table] + [Fast(piece) for piece in [own_values] * split + early],
        [sds((chunks, heads, span, CHUNK), BF16)] + passed,
        [like(logit_table), vmem((chunks, heads, span, CHUNK), BF16)],
    )
    later = [beside(piece, 2) for piece in later]
    chain.space()
    *near, joined = chain.run(
        "gather_gate",
        lambda *args: gather_kernel(parts, *args),
        [Fast(piece) for piece in [own_values] + near + early + later],
        [Fast(sds(own_values.shape, BF16))] * (count // 2) + [sds(own_values.shape, BF16)],
        [vmem((rows * part, span), BF16)] * split,
    )
    other_values = lax.all_gather(joined, "seq", axis=0)
    blocks = [part for piece in near for part in (piece, swap(piece, 1, count))]

    share = 2 * part
    order = list(range(count))
    bare = vmem((tokens, width), F32)
    low = vmem((tokens, width), BF16)
    n_small = 4 + hidden_units // width
    n_small += -n_small % 8
    (
        att_low, second, act, pre_grad, branch, grads_turned, act_kept, hidden1, hidden1_grad, small2, *grad_shares
    ) = chain.run(
        "core",
        lambda *args: core_kernel(heads, segs, parts, order, *args),
        [
            weights, inputs, out_weight, out_bias, ln2_gain, ln2_bias, up_weight, up_bias, cotangent, down_weight,
            *(Fast(block) for block in blocks),
        ],
        [
            Fast(sds((tokens, width), BF16)),
            Fast(sds((tokens, width), BF16)),
            Fast(sds((tokens, hidden_units), BF16)),
            Fast(sds((tokens, hidden_units), BF16)),
            Fast(sds((tokens, width), BF16)),
            Fast(sds((rows * width, span), BF16)),
            sds((tokens, hidden_units), BF16),
            sds((tokens, width), F32),
            sds((tokens, width), F32),
            sds((n_small, width), F32),
        ]
        + [Fast(sds((span, share + LANES), BF16))] * parts,
        [
            like(weights), like(inputs), like(out_weight), like(out_bias), like(ln2_gain), like(ln2_bias),
            like(up_weight), like(up_bias), like(cotangent), like(down_weight),
            vmem((rows, width, full + CHUNK), BF16),
            vmem((rows, WINDOW, CHUNK), BF16),
            vmem((heads, rows * LANES, CHUNK), BF16),
            vmem((heads, span, rows * LANES), F32),
            vmem((rows, heads, span, LANES), F32),
            bare, bare, bare, bare,
            vmem((tokens, hidden_units), F32),
            vmem((tokens, hidden_units), F32),
            bare,
            vmem((span, rows * width), BF16),
            vmem((n_small, width), F32),
        ],
        meta=lengths,
        copies=64,
    )
    shares = [grad_shares[0]] + [beside(grad_shares[t], t) for t in range(1, parts)]
    chain.space()

    upstream = cotangent.reshape(tokens, width)
    narrow = width // count
    size = hidden_units // count
    padded = size + narrow + -(size + narrow) % 32
    send, keep = chain.run(
        "down_grad",
        lambda *args: down_grad_kernel(count, narrow, *args),
        [upstream, Fast(act), Fast(att_low), Fast(branch)],
        [Fast(sds((count // 2, padded, width), BF16))] * 2,
        [low, vmem((width, width), F32)],
    )
    down = Scatter(chain, "down", send, keep, count)
    chain.space()
    send, keep = chain.run(
        "up_value",
        lambda *args: up_value_kernel(heads, segs, count, *args),
        [weights, Fast(pre_grad), Fast(second), Fast(grads_turned)],
        [Fast(sds((count // 2, size + tokens, width), BF16))] * 2,
        [
            like(weights),
            vmem((heads, rows * HALF, span), BF16),
            vmem((rows, width, full), BF16),
            vmem((count, rows * width, span), BF16),
        ],
        meta=lengths,
    )
    up = Scatter(chain, "up", send, keep, count)
    chain.space("long_space")
    (shares,) = chain.run(
        "share_gate",
        share_kernel,
        [Fast(piece) for piece in shares],
        [sds((parts,) + shares[0].shape, BF16)],
    )
    down.step()
    up.step()
    chain.space()

    (logit_part,) = chain.run(
        "logit",
        lambda *args: logit_kernel(each, segs, parts, count, *args),
        [weights, other_values, shares],
        [Fast(sds((chunks, each, span, CHUNK), BF16))],
        [
            vmem((rows * width, full + CHUNK), BF16),
            vmem((2, rows, WINDOW, CHUNK), BF16),
            vmem((2, each, rows * LANES, CHUNK), BF16),
            vmem((2, each, span, rows * LANES), BF16),
            vmem((chunks, each, span, CHUNK), F32),
            vmem((chunks, each, span, CHUNK), BF16),
            vmem(shares.shape, BF16),
            vmem((parts, 8, LANES), jnp.int32),
            pltpu.SMEM((parts, 8, LANES), jnp.int32),
        ],
        meta=lengths,
    )
    logit_grad = []

    def spread(pieces, place_of, picks=(0, 0), onward=0):
        results = chain.run(
            "spread",
            lambda *args: spread_kernel(len(pieces), place_of, picks, *args),
            [Fast(piece) for piece in pieces] + logit_grad,
            [sds((heads, span, full), F32)] + [Fast(sds(pieces[0].shape, BF16))] * onward,
            [vmem((each, span, full), F32)],
            copies=each,
            aliases={len(pieces): 0} if logit_grad else None,
        )
        logit_grad[:] = results[:1]
        return list(results[1:])

    def between(piece):
        return lax.ppermute(piece, "dp", [(1, 2), (2, 1)])

    def outward(piece):
        return lax.ppermute(piece, "dp", [(1, 0), (2, 3)])

    levels = count.bit_length() - 3
    if split:
        near_piece, far_piece = beside(logit_part, 1), between(logit_part)
        down.step(hold=True)
        spread([logit_part], lambda member: member)
    else:
        down.step(hold=True)
        spread([lax.psum(logit_part, "dp")], None)
    for unused in range(levels):
        up.step()
    if split:
        near_piece, far_piece = spread([near_piece, far_piece], lambda member: member ^ 1, (0, 0), 2)
        near_on, far_on = between(near_piece), outward(far_piece)
    layer_out = layer(chain, act, down_weight, hidden1, down_bias).reshape(rows, span, width)
    up, values_grad = up.last([size, tokens])
    up = Across(chain, "up", up, groups)
    down.release()
    for unused in range(levels - 1):
        down.step()
    down = Across(chain, "down", *down.last(), groups)

    extra_rows = n_small + 2
    extra_rows += -extra_rows % 16
    extra_rows += -(narrow + extra_rows) % 32
    input_grad, value_send, value_keep = chain.run(
        "tail",
        lambda *args: tail_kernel(heads, count, *args),
        [
            Fast(values_grad),
            inputs,
            first,
            hidden1_grad,
            ln1_gain,
            value_weight,
            small2,
        ],
        [sds((rows, span, width), F32)]
        + [Fast(sds((count // 2, narrow + extra_rows, width), BF16))] * 2,
        [like(inputs), low, bare, like(ln1_gain), like(value_weight), like(small2)]
        + [
            low,
            vmem((width, width), F32),
            vmem((extra_rows, width), F32),
            vmem((rows, span, width), F32),
        ],
    )
    value = Scatter(chain, "value", value_send, value_keep, count)
    if split:
        (near_on,) = spread(
            [far_piece, far_on, near_on], lambda member: 2 - member // 2, (1, 0), 1
        )
        near_out = outward(near_on)
    up.step()
    down.step()
    value.step()
    up.step()
    for unused in range(levels):
        value.step()
    if split:
        spread([near_on, near_out], lambda member: 3 - 3 * (member // 2), (1, 0))
    value = Across(chain, "value", *value.last(), groups)
    down.step()
    value.step()
    (up_weight_grad,) = up.finish(((size, True),))
    value.step()
    down_weight_grad, out_weight_grad = down.finish(((size, False), (narrow, False)))
    value_weight_grad, small = value.finish(((narrow, False), (extra_rows, False)))

    def mine(vector):
        length = vector.shape[0] // count
        return lax.dynamic_slice_in_dim(vector, here * length, length, 0)

    return (
        layer_out,
        input_grad,
        mine(small[0]),
        mine(small[1]),
        value_weight_grad,
        out_weight_grad,
        mine(small[5]),
        mine(small[3]),
        mine(small[4]),
        up_weight_grad,
        mine(small[6 : 6 + hidden_units // width].reshape(hidden_units)),
        down_weight_grad,
        mine(small[2]),
        logit_grad[0],
    )


def gate_kernel(meta, ins, outs, scratch, move):
    for source, target in zip(ins, outs):
        target[...] = source[...]


def gate(chain, name, arrays):
    return chain.run(
        name,
        gate_kernel,
        [Fast(array) for array in arrays],
        [Fast(sds(array.shape, array.dtype)) for array in arrays],
    )


def layer(chain, act, down_weight, hidden1, down_bias):
    (out,) = chain.run(
        "layer",
        layer_kernel,
        [act, down_weight, hidden1, down_bias],
        [sds(hidden1.shape, BF16)],
        [like(act), like(down_weight), like(hidden1), like(down_bias), like(hidden1, BF16)],
    )
    return out


def solution(mesh):
    return jax.shard_map(
        local,
        mesh=mesh,
        in_specs=(
            P("dp", "seq", None),
            P("dp", None),
            P(),
            P(),
            P(),
            P(),
            P(),
            P(),
            P(),
            P(),
            P(),
            P(),
            P(),
            P(None, "seq", None),
            P("dp", "seq", None),
        ),
        out_specs=(
            P("dp", "seq", None),
            P("dp", "seq", None),
            P("seq"),
            P("seq"),
            P("seq", None),
            P("seq", None),
            P("seq"),
            P("seq"),
            P("seq"),
            P(None, "seq"),
            P("seq"),
            P("seq", None),
            P("seq"),
            P(None, "seq", None),
        ),
        check_vma=False,
    )
```

```python
import math

import jax
import jax.numpy as jnp
from jax import lax
from jax.experimental import pallas as pl
from jax.experimental.pallas import tpu as pltpu
from jax.sharding import PartitionSpec as P

EPSILON = 1e-05
CHUNK = 256
WINDOW = 384
LANES = 128
HALF = 64
GELU_SCALE = math.sqrt(2.0 / math.pi)
GELU_CUBE = 0.044715
F32 = jnp.float32
BF16 = jnp.bfloat16


EXPECTED = {
    "prep": 30,
    "table_exp": 30,
    "core": 200,
    "down_grad": 30,
    "up_value": 100,
    "logit": 160,
    "tail": 3.3,
    "layer": 20,
    "spread": 1.2,
    "space": 20,
    "long_space": 100,
}


def expected(name):
    micros = EXPECTED.get(name, 0.6)
    return pl.CostEstimate(flops=int(micros * 1.15e9), bytes_accessed=1000, transcendentals=0)


def sds(shape, dtype):
    return jax.ShapeDtypeStruct(tuple(shape), dtype)


def dot(left, right):
    return jnp.dot(left, right, preferred_element_type=F32)


def dot_nt(left, right):
    return lax.dot_general(left, right, (((1,), (1,)), ((), ())), preferred_element_type=F32)


def dot_tn(left, right):
    return lax.dot_general(left, right, (((0,), (0,)), ((), ())), preferred_element_type=F32)


def iota(shape, axis):
    return lax.broadcasted_iota(jnp.int32, shape, axis)


def standardize(values_in):
    center = values_in - jnp.mean(values_in, axis=-1, keepdims=True)
    inverse = lax.rsqrt(jnp.mean(center * center, axis=-1, keepdims=True) + EPSILON)
    return (center * inverse, inverse)


def norm_backward(upstream, normed, inverse):
    return inverse * (
        upstream
        - jnp.mean(upstream, axis=-1, keepdims=True)
        - normed * jnp.mean(upstream * normed, axis=-1, keepdims=True)
    )


class Fast:
    def __init__(self, array):
        self.array = array


GRANTS = {
    "prep": 58,
    "table_exp": 58,
    "core": 54,
    "down_grad": 16,
    "up_value": 30,
    "logit": 58,
}


def grant(name, scratch):
    need = 6 * 1024 * 1024
    for piece in scratch:
        if piece.memory_space == pltpu.VMEM:
            need += math.prod(piece.shape) * jnp.dtype(piece.dtype).itemsize * 5 // 4
    least = GRANTS.get(name, 10) * 1024 * 1024
    return pltpu.CompilerParams(vmem_limit_bytes=min(max(least, need), 60 * 1024 * 1024))


class Chain:
    def __init__(self):
        self.token = None

    def space(self, name="space"):
        self.run(name, lambda *unused: None, [], [])

    def run(self, name, body, ins, outs, scratch=(), meta=None, copies=32, chained=True, aliases=None):
        fast_in = [isinstance(piece, Fast) for piece in ins]
        fast_out = [isinstance(piece, Fast) for piece in outs]
        ins = [piece.array if isinstance(piece, Fast) else piece for piece in ins]
        outs = [piece.array if isinstance(piece, Fast) else piece for piece in outs]
        token = [] if self.token is None or not chained else [self.token]
        spaces = {True: pltpu.VMEM, False: pltpu.HBM}
        n_meta, n_in, n_out = int(meta is not None), len(ins), len(outs)

        def kernel(*refs):
            refs = list(refs)
            meta_ref = refs.pop(0) if n_meta else None
            in_refs = refs[:n_in]
            del refs[: n_in + len(token)]
            out_refs = refs[:n_out]
            del refs[: n_out + 1]
            sems = refs.pop()
            used = []

            def move(source, target):
                copy = pltpu.make_async_copy(source, target, sems.at[len(used)])
                used.append(copy)
                copy.start()
                return copy

            body(meta_ref, in_refs, out_refs, refs, move)

        results = pl.pallas_call(
            kernel,
            out_shape=tuple(outs) + (sds((8, LANES), F32),),
            in_specs=[pl.BlockSpec(memory_space=pltpu.SMEM)] * n_meta
            + [pl.BlockSpec(memory_space=spaces[fast]) for fast in fast_in]
            + [pl.BlockSpec(memory_space=pl.ANY)] * len(token),
            out_specs=[pl.BlockSpec(memory_space=spaces[fast]) for fast in fast_out]
            + [pl.BlockSpec(memory_space=pl.ANY)],
            scratch_shapes=list(scratch) + [pltpu.SemaphoreType.DMA((copies,))],
            input_output_aliases={n_meta + at: to for at, to in (aliases or {}).items()},
            compiler_params=grant(name, scratch),
            cost_estimate=expected(name),
            name=name,
        )(*([meta] if n_meta else []), *ins, *token)
        if chained:
            self.token = results[-1]
        return results[:-1]


def vmem(shape, dtype):
    return pltpu.VMEM(tuple(shape), dtype)


def like(array, dtype=None):
    return pltpu.VMEM(tuple(array.shape), dtype or array.dtype)


def segment(lengths, index, segs):
    start = jnp.int32(0)
    for at in range(segs):
        start = start + jnp.where(at < index, lengths[at], 0)
    return (start, jnp.where(index < segs, lengths[jnp.minimum(index, segs - 1)], 0))


class RowLengths:
    def __init__(self, ref, row):
        self.ref, self.row = ref, row

    def __getitem__(self, index):
        return self.ref[self.row, index]


class Lengths:
    def __init__(self, ref, source, base):
        self.ref, self.source, self.base = ref, source, base

    def __getitem__(self, index):
        return self.ref[self.source, 0, HALF + 2 * (self.base + index)]


def first_segment(lengths, place, segs):
    index, end = jnp.int32(0), jnp.int32(0)
    for at in range(segs):
        end = end + lengths[at]
        index = index + jnp.where(end <= place, 1, 0)
    return index


def overlapped(lengths, index, begin, end, segs):
    start, length = segment(lengths, index, segs)
    touches = (start < end) & (start + length > begin)
    return (jnp.where(touches, start, 0), jnp.where(touches, length, 0))


def chunk_count(lengths):
    longest = lengths[0]
    for length in lengths[1:]:
        longest = jnp.maximum(longest, length)
    return (longest + CHUNK - 1) // CHUNK


def shifter(start):
    hit = iota((WINDOW, CHUNK), 0) == iota((WINDOW, CHUNK), 1) + lax.rem(start, LANES)
    return hit.astype(F32).astype(BF16)


def shifted(values_ref, rows, move_ref, start, length, at):
    window = jnp.minimum((start // LANES) * LANES + at * CHUNK, values_ref.shape[1] - WINDOW)
    window = pl.multiple_of(window, LANES)
    mover = jnp.where(iota((WINDOW, CHUNK), 1) < length - at * CHUNK, move_ref[...], 0)
    return dot(values_ref[rows, pl.ds(window, WINDOW)], mover)


def row_blocks(count):
    return [slice(at, at + 16) for at in range(0, count, 16)]


def put_shares(values, target, offsets, rows, groups):
    width = values.shape[0] // rows
    part = width // groups
    for at, offset in enumerate(offsets):
        owner = lax.axis_index("dp") ^ offset
        for row in range(rows):
            begin = pl.multiple_of(row * width + owner * part, HALF)
            spot = (at * rows + row) * part
            target[spot : spot + part] = values[pl.ds(begin, part)]


def prep_kernel(groups, meta, ins, outs, scratch, move):
    x_ref, gain_ref, bias_ref, weight_ref, first_ref = scratch
    loads = [move(*pair) for pair in zip(ins, scratch)]
    rows, span, width = x_ref.shape
    for load in loads[:3]:
        load.wait()
    xhat, unused = standardize(x_ref[...].reshape(rows * span, width).astype(F32))
    first_ref[...] = (xhat * gain_ref[...] + bias_ref[...]).astype(BF16)
    store = move(first_ref, outs[0])
    loads[3].wait()
    turned = dot(first_ref[...], weight_ref[...]).T.astype(BF16)
    values = outs[1]
    for row in range(rows):
        values[row * width : (row + 1) * width] = turned[:, row * span : (row + 1) * span]
    if groups > 1:
        put_shares(values, outs[2], (1, 3), rows, groups)
    store.wait()


def exp_kernel(groups, meta, ins, outs, scratch, move):
    table_ref, e_ref = scratch
    chunks, heads = e_ref.shape[:2]
    loads = [move(ins[0].at[head], table_ref.at[head]) for head in range(heads)]
    stores = []
    for head in range(heads):
        loads[head].wait()
        e = jnp.exp(table_ref[head].astype(F32)).astype(BF16)
        for at in range(chunks):
            e_ref[at, head] = e[:, at * CHUNK : (at + 1) * CHUNK]
        stores.append(move(e_ref.at[:, head], outs[0].at[:, head]))
    if groups > 1:
        values, got = ins[1:]
        half = got.shape[0] // 2
        put_shares(values, outs[1], (2,), 2, groups)
        outs[1][half:] = got[half:]
    for store in stores:
        store.wait()


def gather_kernel(groups, meta, ins, outs, scratch, move):
    near = ins[: len(outs) - 1]
    joined = outs[-1]
    if groups > 1:
        (own_ref,) = scratch
        first, second = ins[len(near) :]
        put_shares(ins[0], own_ref, (0,), 2, groups)
        size = own_ref.shape[0]
        copies = [
            move(own_ref, joined.at[pl.ds(0, size)]),
            move(first.at[pl.ds(0, size)], joined.at[pl.ds(size, size)]),
            move(second, joined.at[pl.ds(2 * size, 2 * size)]),
        ]
    else:
        copies = [move(ins[0], joined)]
    for source, target in zip(near, outs):
        target[...] = source[...]
    for copy in copies:
        copy.wait()


def share_kernel(meta, ins, outs, scratch, move):
    copies = [move(piece, outs[0].at[at]) for at, piece in enumerate(ins)]
    for copy in copies:
        copy.wait()


def core_kernel(heads, segs, groups, order, meta, ins, outs, scratch, move):
    (
        e_ref, x_ref, outw_ref, outb_ref, gain_ref, bias_ref, up_ref, upb_ref, g_ref, down_ref,
        values_ref, move_ref, aug_ref, acc_ref, res_ref, att_ref, tot_ref, h1_ref, back_ref, raw_ref,
        back_in_ref, h1_grad_ref, paired_ref, small_ref,
    ) = scratch
    low_ref, second_ref, act_ref, pre_ref, branch_ref, turned_out, act_out, h1_out, h1_grad_out, small_out = outs[:10]
    share_out = outs[10:]
    rows, span, width = x_ref.shape
    hidden_units = up_ref.shape[1]
    here = lax.axis_index("seq")
    blocks = ins[10:]
    loads = [move(*pair) for pair in zip(ins[:10], scratch[:10])]
    later = loads[1:]
    for at, offset in enumerate(order):
        place = pl.multiple_of((here ^ offset) * span, LANES)
        for row in range(rows):
            values_ref[row, :, pl.ds(place, span)] = blocks[at][row * width : (row + 1) * width]
    full = values_ref.shape[2] - CHUNK
    values_ref[:, :, full:] = jnp.zeros((rows, width, CHUNK), BF16)
    res_ref[...] = jnp.zeros_like(res_ref)
    begin, end = here * span, (here + 1) * span
    places = begin + iota((span, LANES), 0)
    lengths = [RowLengths(meta, row) for row in range(rows)]
    firsts = [first_segment(lengths[row], begin, segs) for row in range(rows)]
    loads[0].wait()

    def slot(turn, carry):
        bounds = [
            overlapped(lengths[row], firsts[row] + turn, begin, end, segs) for row in range(rows)
        ]
        count = chunk_count([length for unused, length in bounds])

        @pl.when(count > 0)
        def _():
            acc_ref[...] = jnp.zeros_like(acc_ref)
            for row, (start, unused) in enumerate(bounds):
                move_ref[row] = shifter(start)

            def chunk(at, state):
                for row, (start, length) in enumerate(bounds):
                    moved = shifted(
                        values_ref.at[row], slice(None), move_ref.at[row], start, length, at
                    ).astype(BF16)
                    ones = iota((HALF, CHUNK), 1) < length - at * CHUNK
                    ones = ones.astype(F32).astype(BF16)
                    for head in range(heads):
                        base = row * LANES
                        spots = (base, base + HALF) if head % 2 == 0 else (base + HALF, base)
                        aug_ref[head, spots[0] : spots[0] + HALF] = moved[head * HALF : (head + 1) * HALF]
                        aug_ref[head, spots[1] : spots[1] + HALF] = ones
                for head in range(heads):
                    acc_ref[head] += dot_nt(e_ref[at, head], aug_ref[head])
                return state

            lax.fori_loop(0, count, chunk, 0)
            for row, (start, length) in enumerate(bounds):
                inside = (places >= start) & (places < start + length)
                for head in range(heads):
                    res_ref[row, head] = jnp.where(
                        inside, acc_ref[head, :, row * LANES : (row + 1) * LANES], res_ref[row, head]
                    )

        return carry

    lax.fori_loop(0, segs, slot, 0)
    low_lanes = iota((span, LANES), 1) < HALF
    for row in range(rows):
        for pair in range(heads // 2):
            even, odd = res_ref[row, 2 * pair], res_ref[row, 2 * pair + 1]
            total = pltpu.roll(jnp.where(low_lanes, odd, even), HALF, 1)
            attended = jnp.where(low_lanes, even, odd) / total
            spot = (slice(row * span, (row + 1) * span), slice(pair * LANES, (pair + 1) * LANES))
            tot_ref[spot] = total
            att_ref[spot] = attended
            low_ref[spot] = attended.astype(BF16)
    stores = []
    for load in later:
        load.wait()
    tokens = rows * span
    blocks = row_blocks(tokens)
    h1_ref[...] = dot(low_ref[...], outw_ref[...])
    for spot in blocks:
        row, at = spot.start // span, spot.start % span
        hidden = h1_ref[spot] + x_ref[row, at : at + 16].astype(F32) + outb_ref[...]
        h1_ref[spot] = hidden
        xhat2, unused = standardize(hidden)
        second_ref[spot] = (xhat2 * gain_ref[...] + bias_ref[...]).astype(BF16)
    stores.append(move(h1_ref, h1_out))

    small_ref[...] = jnp.zeros_like(small_ref)
    g_low = g_ref[...].reshape(tokens, width)
    for index in range(hidden_units // width):
        cols = slice(index * width, (index + 1) * width)
        raw_ref[:, cols] = dot(second_ref[...], up_ref[:, cols])
        back_in_ref[:, cols] = dot_nt(g_low, down_ref[cols])
    half_width = width // 2
    for index in range(hidden_units // width):
        cols = slice(index * width, (index + 1) * width)
        for part in range(2):
            thin = slice(cols.start + part * half_width, cols.start + (part + 1) * half_width)
            upb = upb_ref[thin]
            tally = jnp.zeros((8, half_width), F32)
            for spot in blocks:
                pre = raw_ref[spot, thin] + upb
                square = pre * pre
                bent = jnp.tanh(pre * (GELU_SCALE + (GELU_SCALE * GELU_CUBE) * square))
                half = 0.5 + 0.5 * bent
                act_ref[spot, thin] = (pre * half).astype(BF16)
                slope = half + (pre * (half - half * bent)) * (
                    GELU_SCALE + (3.0 * GELU_SCALE * GELU_CUBE) * square
                )
                pre_grad = (back_in_ref[spot, thin] * slope).astype(BF16)
                pre_ref[spot, thin] = pre_grad
                wide = pre_grad.astype(F32)
                tally = tally + wide[:8] + wide[8:]
            small_ref[4 + index : 5 + index, part * half_width : (part + 1) * half_width] = jnp.sum(
                tally, axis=0, keepdims=True
            )
        stores.append(move(act_ref.at[:, cols], act_out.at[:, cols]))
        back = dot_nt(pre_ref[:, cols], up_ref[:, cols])
        back_ref[...] = back if index == 0 else back_ref[...] + back

    tallies = [jnp.zeros((8, width), F32)] * 4
    for spot in blocks:
        row, at = spot.start // span, spot.start % span
        back = back_ref[spot]
        wide = g_ref[row, at : at + 16].astype(F32)
        xhat2, inverse2 = standardize(h1_ref[spot])
        hidden_grad = wide + norm_backward(back * gain_ref[...], xhat2, inverse2)
        h1_grad_ref[spot] = hidden_grad
        branch = hidden_grad.astype(BF16)
        branch_ref[spot] = branch
        terms = (wide, back * xhat2, back, branch.astype(F32))
        tallies = [tally + term[:8] + term[8:] for tally, term in zip(tallies, terms)]
    for index, tally in enumerate(tallies):
        small_ref[index : index + 1] = jnp.sum(tally, axis=0, keepdims=True)
    stores.append(move(small_ref, small_out))
    stores.append(move(h1_grad_ref, h1_grad_out))
    att_grad = dot_nt(branch_ref[...], outw_ref[...])
    scaled = att_grad / tot_ref[...]
    weigh = scaled * att_ref[...]
    pick = (iota((width, LANES), 1) == 4 * (iota((width, LANES), 0) // HALF)).astype(F32).astype(BF16)
    high = weigh.astype(BF16)
    rest = (weigh - high.astype(F32)).astype(BF16)
    offset = dot(high, pick) + dot(rest, pick)
    rounded = offset.astype(BF16).astype(F32)
    offset = rounded + pltpu.roll(offset - rounded, 1, 1)
    offsets = offset[:span] + pltpu.roll(offset[span:], 2, 1)
    codes = jnp.zeros((span, LANES), F32)
    lane = iota((span, LANES), 1)
    for index in range(rows * segs):
        length = meta[index // segs, index % segs]
        codes = jnp.where(lane == HALF + 2 * index, (length // HALF).astype(F32), codes)
        codes = jnp.where(lane == HALF + 2 * index + 1, lax.rem(length, HALF).astype(F32), codes)
    scaled0, scaled1 = scaled[:span], scaled[span:]
    for pair in range(heads // 2):
        part0 = scaled0[:, pair * LANES : (pair + 1) * LANES]
        part1 = scaled1[:, pair * LANES : (pair + 1) * LANES]
        even = jnp.where(low_lanes, part0, pltpu.roll(part1, HALF, 1))
        odd = jnp.where(low_lanes, pltpu.roll(part0, HALF, 1), part1)
        paired_ref[:, 2 * pair * LANES : (2 * pair + 1) * LANES] = even.astype(BF16)
        paired_ref[:, (2 * pair + 1) * LANES : (2 * pair + 2) * LANES] = odd.astype(BF16)
    part = 2 * width // groups
    each = heads // groups
    group = lax.axis_index("dp") if groups > 1 else 0
    for turn in range(groups):
        owner = group ^ turn
        begin_lane = pl.multiple_of(owner * part, LANES)
        share_out[turn][:, :part] = paired_ref[:, pl.ds(begin_lane, part)]
        spin = lax.rem(LANES - 4 * each * owner, LANES)
        spun = pltpu.roll(offsets, spin, 1)
        share_out[turn][:, part:] = jnp.where(lane < HALF, spun, codes).astype(BF16)
    for row, piece in enumerate((scaled0, scaled1)):
        turned_out[row * width : (row + 1) * width] = piece.T.astype(BF16)
    for store in stores:
        store.wait()


def value_part_kernel(heads, segs, count, base, grads_ref, e_ref, lhs_ref, part_ref, acc_ref, send, keep, meta):
    rows = 2
    span = grads_ref.shape[1]
    width = grads_ref.shape[0] // rows
    here = lax.axis_index("seq")
    begin, end = here * span, (here + 1) * span
    acc_ref[...] = jnp.zeros_like(acc_ref)
    places = begin + iota((HALF, span), 1)
    lengths = [RowLengths(meta, row) for row in range(rows)]
    firsts = [first_segment(lengths[row], begin, segs) for row in range(rows)]

    def slot(turn, carry):
        bounds = [
            overlapped(lengths[row], firsts[row] + turn, begin, end, segs) for row in range(rows)
        ]
        chunks = chunk_count([length for unused, length in bounds])

        @pl.when(chunks > 0)
        def _():
            for row, (start, length) in enumerate(bounds):
                inside = (places >= start) & (places < start + length)
                for head in range(heads):
                    spot = row * width + head * HALF
                    piece = grads_ref[spot : spot + HALF].astype(F32)
                    lhs_ref[head, row * HALF : (row + 1) * HALF] = jnp.where(inside, piece, 0.0).astype(BF16)

            def chunk(at, state):
                cols = pl.ds(pl.multiple_of(at * CHUNK, CHUNK), CHUNK)
                for head in range(heads):
                    piece = dot(lhs_ref[head], e_ref[at, head]).astype(BF16)
                    for row in range(rows):
                        part_ref[row, head * HALF : (head + 1) * HALF, cols] = piece[
                            row * HALF : (row + 1) * HALF
                        ]
                return state

            lax.fori_loop(0, chunks, chunk, 0)
            limit = chunks * CHUNK - 2 * LANES
            for row, (start, length) in enumerate(bounds):

                def tile(at, state):
                    first = at * LANES - start
                    window = jnp.clip(((first + count * span) // LANES) * LANES - count * span, 0, limit)
                    window = pl.multiple_of(window, LANES)
                    column = iota((2 * LANES, LANES), 1) + first
                    hit = (iota((2 * LANES, LANES), 0) + window == column) & (column < length)
                    moved = dot(
                        part_ref[row, :, pl.ds(window, 2 * LANES)], hit.astype(F32).astype(BF16)
                    )
                    acc_ref[at, row * width : (row + 1) * width] += moved.astype(BF16)
                    return state

                last = jnp.where(length > 0, (start + length + LANES - 1) // LANES, 0)
                lax.fori_loop(start // LANES, last, tile, 0)

        return carry

    lax.fori_loop(0, segs, slot, 0)
    high = rows * span
    for at in range(count // 2):
        for odd, target in ((1, send), (0, keep)):
            for index in range(rows * width // high):
                target[at, base : base + high, index * span : (index + 1) * span] = acc_ref[
                    here ^ (2 * at + odd), index * high : (index + 1) * high
                ]


def logit_kernel(heads, segs, groups, count, meta, ins, outs, scratch, move):
    weights, values, shares = ins
    values_ref, move_ref, aug_ref, lhs_ref, acc_ref, e_ref, stage_all, codes_ref, lens_ref = scratch
    rows = 2
    span = shares.shape[1]
    half = heads * HALF
    part = heads * LANES
    here = lax.axis_index("seq")
    group = lax.axis_index("dp") if groups > 1 else 0
    share_load = move(shares, stage_all)
    e_load = move(weights.at[:, pl.ds(group * heads, heads)], e_ref)
    loads = [
        move(values.at[at], values_ref.at[:, at * span : (at + 1) * span]) for at in range(count)
    ]
    acc_ref[...] = jnp.zeros_like(acc_ref)
    values_ref[:, count * span :] = jnp.zeros((values_ref.shape[0], CHUNK), BF16)
    begin, end = here * span, (here + 1) * span
    places = begin + iota((span, LANES), 0)
    lane = iota((span, LANES), 1)
    share_load.wait()
    for source in range(groups):
        parts = stage_all[source, :16, part:].astype(F32)
        whole = HALF * parts + pltpu.roll(parts, LANES - 1, 1)
        codes_ref[source] = whole[:8].astype(jnp.int32)
    loads.append(move(codes_ref, lens_ref))
    for load in loads:
        load.wait()

    def slot(sources, turn, carry):
        all_bounds = []
        for source in sources:
            bounds = []
            for row in range(rows):
                lens = Lengths(lens_ref, source, row * segs)
                index = first_segment(lens, begin, segs) + turn
                bounds.append(overlapped(lens, index, begin, end, segs))
            all_bounds.append(bounds)
        chunks = chunk_count([length for bounds in all_bounds for unused, length in bounds])

        @pl.when(chunks > 0)
        def _():
            for number, (source, bounds) in enumerate(zip(sources, all_bounds)):
                offsets = stage_all[source, :, part:].astype(F32)
                for row, (start, length) in enumerate(bounds):
                    move_ref[number, row] = shifter(start)
                    inside = (places >= start) & (places < start + length)
                    for head in range(heads):
                        grad = stage_all[source, :, head * LANES : (head + 1) * LANES].astype(F32)
                        if row == 1:
                            grad = pltpu.roll(grad, HALF, 1)
                        fill = pltpu.roll(offsets, (HALF - 4 * head - 2 * row) % LANES, 1)
                        fill = jnp.where((lane == HALF) | (lane == HALF + 1), -fill, 0.0)
                        lhs = jnp.where(inside, jnp.where(lane < HALF, grad, fill), 0.0)
                        lhs_ref[number, head, :, row * LANES : (row + 1) * LANES] = lhs.astype(BF16)

            def chunk(at, state):
                for number, (source, bounds) in enumerate(zip(sources, all_bounds)):
                    for row, (start, length) in enumerate(bounds):
                        place = (source * rows + row) * half
                        moved = shifted(
                            values_ref,
                            slice(place, place + half),
                            move_ref.at[number, row],
                            start,
                            length,
                            at,
                        ).astype(BF16)
                        ones = iota((HALF, CHUNK), 1) < length - at * CHUNK
                        ones = ones.astype(F32).astype(BF16)
                        for head in range(heads):
                            base = row * LANES
                            aug_ref[number, head, base : base + HALF] = moved[head * HALF : (head + 1) * HALF]
                            aug_ref[number, head, base + HALF : base + LANES] = ones
                for head in range(heads):
                    total = acc_ref[at, head]
                    for number in range(len(sources)):
                        total = total + dot(lhs_ref[number, head], aug_ref[number, head])
                    acc_ref[at, head] = total
                return state

            lax.fori_loop(0, chunks, chunk, 0)

        return carry

    for first in range(0, groups, 2):
        sources = list(range(first, min(first + 2, groups)))
        lax.fori_loop(0, segs, lambda turn, carry: slot(sources, turn, carry), 0)
    e_load.wait()
    outs[0][...] = (acc_ref[...] * e_ref[...].astype(F32)).astype(BF16)


def spread_kernel(count, place_of, picks, meta, ins, outs, scratch, move):
    (out_ref,) = scratch
    member = lax.axis_index("dp") if place_of else 0
    place = place_of(member) if place_of else 0
    pieces = ins[:count]
    chunks, heads = pieces[0].shape[:2]
    for source, target in zip(pieces[len(pieces) - len(outs) + 1 :], outs[1:]):
        target[...] = source[...]
    outer = (member == 0) | (member == 3)
    stores = []
    for head in range(heads):
        for at in range(chunks):
            values = pieces[picks[0]][at, head]
            if picks[0] != picks[1]:
                values = jnp.where(outer, values, pieces[picks[1]][at, head])
            out_ref[head, :, at * CHUNK : (at + 1) * CHUNK] = values.astype(F32)
        stores.append(move(out_ref.at[head], outs[0].at[place * heads + head]))
    for store in stores:
        store.wait()


def cut_rows(full_ref, index, size):
    return full_ref[pl.ds(pl.multiple_of(index * size, 16), size), :].astype(BF16)


def cut_product(count, left_ref, right, send, keep, here):
    size = left_ref.shape[1] // count
    for at in range(count // 2):
        for odd, target in ((1, send), (0, keep)):
            member = here ^ (2 * at + odd)
            if size % LANES == 0:
                left = left_ref[:, pl.ds(pl.multiple_of(member * size, LANES), size)]
                target[at, :size] = dot_tn(left, right).astype(BF16)
                continue
            wide = -(-size // LANES) * LANES
            begin = jnp.minimum((member * size // LANES) * LANES, left_ref.shape[1] - wide)
            begin = pl.multiple_of(begin, LANES)
            product = dot_tn(left_ref[:, pl.ds(begin, wide)], right)
            apart = member * size - begin
            for choice in range(0, wide - size + 1, HALF):

                @pl.when(apart == choice)
                def _():
                    target[at, :size] = product[choice : choice + size].astype(BF16)


def down_grad_kernel(count, narrow, meta, ins, outs, scratch, move):
    act_ref, low_ref, branch_ref = ins[1:]
    g_ref, full_ref = scratch
    move(ins[0], g_ref).wait()
    send, keep = outs
    size, padded = act_ref.shape[1] // count, send.shape[1]
    here = lax.axis_index("seq")
    cut_product(count, act_ref, g_ref[...], send, keep, here)
    full_ref[...] = dot_tn(low_ref[...], branch_ref[...])
    for at in range(count // 2):
        for odd, target in ((1, send), (0, keep)):
            target[at, size : size + narrow] = cut_rows(full_ref, here ^ (2 * at + odd), narrow)
            if padded > size + narrow:
                target[at, size + narrow :] = jnp.zeros((padded - size - narrow, target.shape[2]), BF16)


def up_value_kernel(heads, segs, count, meta, ins, outs, scratch, move):
    pre_ref, second_ref, grads_ref = ins[1:]
    e_ref, lhs_ref, part_ref, acc_ref = scratch
    load = move(ins[0], e_ref)
    send, keep = outs
    size = pre_ref.shape[1] // count
    cut_product(count, pre_ref, second_ref[...], send, keep, lax.axis_index("seq"))
    load.wait()
    value_part_kernel(
        heads, segs, count, size, grads_ref, e_ref, lhs_ref, part_ref, acc_ref, send, keep, meta
    )


def layer_kernel(meta, ins, outs, scratch, move):
    act_ref, down_ref, h1_ref, bias_ref, out_ref = scratch
    loads = [move(*pair) for pair in zip(ins, scratch)]
    for load in loads:
        load.wait()
    out_ref[...] = (h1_ref[...] + dot(act_ref[...], down_ref[...]) + bias_ref[...]).astype(BF16)
    move(out_ref, outs[0]).wait()


def tail_kernel(heads, count, meta, ins, outs, scratch, move):
    (
        x_ref, first_ref, h1_grad_ref, gain_ref, weight_ref, small2_ref, grads_ref, full_ref, small_ref, back_ref,
    ) = scratch
    loads = [move(*pair) for pair in zip(ins[1:], scratch)]
    input_grad, send, keep = outs
    rows, span, width = x_ref.shape
    high = rows * span
    for index in range(rows * width // high):
        turned = ins[0][:, index * span : (index + 1) * span].astype(F32).T.astype(BF16)
        row, begin = index * high // width, index * high % width
        grads_ref[row * span : (row + 1) * span, begin : begin + high] = turned
    for load in loads:
        load.wait()
    grads = grads_ref[...]
    full_ref[...] = dot_tn(first_ref[...], grads)
    back = dot_nt(grads, weight_ref[...])
    xhat, inverse = standardize(x_ref[...].reshape(rows * span, width).astype(F32))
    small_ref[...] = jnp.zeros_like(small_ref)
    small_ref[0:1] = jnp.sum(back * xhat, axis=0, keepdims=True)
    small_ref[1:2] = jnp.sum(back, axis=0, keepdims=True)
    small_ref[2 : 2 + small2_ref.shape[0]] = small2_ref[...]
    small = small_ref[...].astype(BF16)
    size = send.shape[1] - small.shape[0]
    here = lax.axis_index("seq")
    for at in range(count // 2):
        for odd, target in ((1, send), (0, keep)):
            target[at, :size] = cut_rows(full_ref, here ^ (2 * at + odd), size)
            target[at, size:] = small
    back_ref[...] = (
        h1_grad_ref[...] + norm_backward(back * gain_ref[...], xhat, inverse)
    ).reshape(rows, span, width)
    move(back_ref, input_grad).wait()


def sum_kernel(jobs, meta, ins, outs, scratch, move):
    for (left, left_at), (right, right_at), routes in jobs:
        for begin, size, target, index, place in routes:
            rows = slice(begin, begin + size)
            left_spot = rows if left_at is None else (left_at, rows)
            right_spot = rows if right_at is None else (right_at, rows)
            total = ins[left][left_spot].astype(F32) + ins[right][right_spot].astype(F32)
            spot = slice(place or 0, (place or 0) + size)
            outs[target][spot if index is None else (index, spot)] = total.astype(BF16)


def finish_kernel(groups, plan, meta, ins, outs, scratch, move):
    middle_ref, outer_ref = ins
    member = lax.axis_index("dp")
    outer = (member == 0) | (member == groups - 1)
    stores = []
    begin = 0
    for number, (size, turned) in enumerate(plan):
        spot = slice(begin, begin + size)
        picked = jnp.where(outer, outer_ref[spot].astype(F32), middle_ref[spot].astype(F32))
        scratch[number][...] = picked.T if turned else picked
        stores.append(move(scratch[number], outs[number]))
        begin += size
    for store in stores:
        store.wait()


def swap(piece, distance, count):
    return lax.ppermute(piece, "seq", [(at, at ^ distance) for at in range(count)])


def beside(piece, distance):
    return lax.ppermute(piece, "dp", [(at, at ^ distance) for at in range(4)])


def add_pieces(chain, name, arrays, jobs, outs):
    return chain.run(
        name,
        lambda *args: sum_kernel(jobs, *args),
        [Fast(array) for array in arrays],
        [Fast(sds(shape, BF16)) for shape in outs],
    )


class Scatter:
    def __init__(self, chain, name, send, keep, count):
        self.chain, self.name, self.count = chain, name, count
        self.keep = keep
        self.bits = list(range(count.bit_length() - 2))
        self.level = 0
        self.got = [swap(send, 1, count)]

    def step(self, hold=False):
        members, rows, width = self.keep.shape if self.level == 0 else self.stay[0].shape
        if self.level == 0:
            half = rows // 2
            outs = [(members // 2, half, width)] * 4
            jobs = []
            for m in range(members):
                a_out = (0 if m & 1 else 1, m >> 1)
                top = m >= members // 2
                b_out = (2 if top else 3, m % (members // 2))
                jobs.append(
                    (
                        (0, m),
                        (1, m),
                        [
                            (0, half, a_out[0], a_out[1], None),
                            (half, half, b_out[0], b_out[1], None),
                        ],
                    )
                )
            results = add_pieces(
                self.chain,
                self.name + "_add0",
                [self.keep, self.got[0]],
                jobs,
                outs,
            )
        else:
            outs = [(members // 2, rows, width)] * 4
            jobs = []
            for side in range(2):
                for m in range(members):
                    if side == 0:
                        spot = (0 if m & 1 else 1, m >> 1)
                    else:
                        spot = (2 if m >= members // 2 else 3, m % (members // 2))
                    jobs.append(
                        (
                            (2 * side, m),
                            (2 * side + 1, m),
                            [(0, rows, spot[0], spot[1], None)],
                        )
                    )
            results = add_pieces(
                self.chain,
                self.name + "_add" + str(self.level),
                [self.stay[0], self.got[0], self.stay[1], self.got[1]],
                jobs,
                outs,
            )
        self.stay = [results[1], results[3]]
        self.going = [results[0], results[2]]
        if not hold:
            self.send()
        return self

    def release(self):
        self.going = gate(self.chain, self.name + "_gate", self.going)
        self.send()

    def send(self):
        self.got = [
            swap(self.going[0], 2 << self.bits[self.level], self.count),
            swap(self.going[1], 2 << self.bits[-1 - self.level], self.count),
        ]
        self.level += 1

    def last(self, cuts=None):
        unused, rows, width = self.stay[0].shape
        cuts = cuts or [2 * rows]
        begins = [sum(cuts[:at]) for at in range(len(cuts))]
        jobs = []
        for side in range(2):
            routes = []
            for number, (begin, size) in enumerate(zip(begins, cuts)):
                low = max(begin, side * rows)
                high = min(begin + size, (side + 1) * rows)
                if low < high:
                    routes.append((low - side * rows, high - low, number, None, low - begin))
            jobs.append(((2 * side, 0), (2 * side + 1, 0), routes))
        return add_pieces(
            self.chain,
            self.name + "_last",
            [self.stay[0], self.got[0], self.stay[1], self.got[1]],
            jobs,
            [(size, width) for size in cuts],
        )


class Across:
    def __init__(self, chain, name, piece, groups):
        self.chain, self.name, self.groups, self.level = chain, name, groups, 0
        self.piece = piece
        if groups == 4:
            self.got = lax.ppermute(piece, "dp", [(0, 1), (3, 2)])

    def step(self):
        if self.groups != 4:
            if self.level == 0:
                self.piece = lax.psum(self.piece, "dp")
                self.got = self.piece
        else:
            shape = self.piece.shape
            self.piece = add_pieces(
                self.chain,
                self.name + "_dp" + str(self.level),
                [self.piece, self.got],
                [((0, None), (1, None), [(0, shape[0], 0, None, None)])],
                [shape],
            )[0]
            pairs = [(1, 2), (2, 1)] if self.level == 0 else [(1, 0), (2, 3)]
            self.got = lax.ppermute(self.piece, "dp", pairs)
        self.level += 1
        return self

    def finish(self, plan):
        shape = self.piece.shape
        outs = [sds((shape[1], size) if turned else (size, shape[1]), F32) for size, turned in plan]
        return self.chain.run(
            self.name + "_finish",
            lambda *args: finish_kernel(self.groups, plan, *args),
            [Fast(self.piece), Fast(self.got)],
            outs,
            [vmem(out.shape, F32) for out in outs],
        )


def local(
    inputs,
    lengths,
    ln1_gain,
    ln1_bias,
    value_weight,
    out_weight,
    out_bias,
    ln2_gain,
    ln2_bias,
    up_weight,
    up_bias,
    down_weight,
    down_bias,
    logit_table,
    cotangent,
):
    rows, span, width = inputs.shape
    heads, unused_span, full = logit_table.shape
    segs = lengths.shape[1]
    hidden_units = up_weight.shape[1]
    tokens = rows * span
    count = lax.axis_size("seq")
    groups = lax.axis_size("dp")
    here = lax.axis_index("seq")
    chunks = full // CHUNK
    split = groups == 4 and heads % groups == 0
    parts = groups if split else 1
    each = heads // parts
    chain = Chain()

    part = width // parts
    passed = [Fast(sds((2 * rows * part, span), BF16))] * split
    first, own_values, *early = chain.run(
        "prep",
        lambda *args: prep_kernel(parts, *args),
        [inputs, ln1_gain, ln1_bias, value_weight],
        [sds((tokens, width), BF16), Fast(sds((rows * width, span), BF16))] + passed,
        [like(inputs), like(ln1_gain), like(ln1_bias), like(value_weight)]
        + [vmem((tokens, width), BF16)],
    )
    near = [swap(own_values, offset, count) for offset in range(2, count, 2)]
    early = [beside(piece, 1) for piece in early]
    weights, *later = chain.run(
        "table_exp",
        lambda *args: exp_kernel(parts, *args),
        [logit_table] + [Fast(piece) for piece in [own_values] * split + early],
        [sds((chunks, heads, span, CHUNK), BF16)] + passed,
        [like(logit_table), vmem((chunks, heads, span, CHUNK), BF16)],
    )
    later = [beside(piece, 2) for piece in later]
    *near, joined = chain.run(
        "gather_gate",
        lambda *args: gather_kernel(parts, *args),
        [Fast(piece) for piece in [own_values] + near + early + later],
        [Fast(sds(own_values.shape, BF16))] * (count // 2) + [sds(own_values.shape, BF16)],
        [vmem((rows * part, span), BF16)] * split,
    )
    other_values = lax.all_gather(joined, "seq", axis=0)
    blocks = [part for piece in near for part in (piece, swap(piece, 1, count))]

    share = 2 * part
    order = list(range(count))
    bare = vmem((tokens, width), F32)
    low = vmem((tokens, width), BF16)
    n_small = 4 + hidden_units // width
    n_small += -n_small % 8
    (
        att_low, second, act, pre_grad, branch, grads_turned, act_kept, hidden1, hidden1_grad, small2, *grad_shares
    ) = chain.run(
        "core",
        lambda *args: core_kernel(heads, segs, parts, order, *args),
        [
            weights, inputs, out_weight, out_bias, ln2_gain, ln2_bias, up_weight, up_bias, cotangent, down_weight,
            *(Fast(block) for block in blocks),
        ],
        [
            Fast(sds((tokens, width), BF16)),
            Fast(sds((tokens, width), BF16)),
            Fast(sds((tokens, hidden_units), BF16)),
            Fast(sds((tokens, hidden_units), BF16)),
            Fast(sds((tokens, width), BF16)),
            Fast(sds((rows * width, span), BF16)),
            sds((tokens, hidden_units), BF16),
            sds((tokens, width), F32),
            sds((tokens, width), F32),
            sds((n_small, width), F32),
        ]
        + [Fast(sds((span, share + LANES), BF16))] * parts,
        [
            like(weights), like(inputs), like(out_weight), like(out_bias), like(ln2_gain), like(ln2_bias),
            like(up_weight), like(up_bias), like(cotangent), like(down_weight),
            vmem((rows, width, full + CHUNK), BF16),
            vmem((rows, WINDOW, CHUNK), BF16),
            vmem((heads, rows * LANES, CHUNK), BF16),
            vmem((heads, span, rows * LANES), F32),
            vmem((rows, heads, span, LANES), F32),
            bare, bare, bare, bare,
            vmem((tokens, hidden_units), F32),
            vmem((tokens, hidden_units), F32),
            bare,
            vmem((span, rows * width), BF16),
            vmem((n_small, width), F32),
        ],
        meta=lengths,
        copies=64,
    )
    shares = [grad_shares[0]] + [beside(grad_shares[t], t) for t in range(1, parts)]
    chain.space()

    upstream = cotangent.reshape(tokens, width)
    narrow = width // count
    size = hidden_units // count
    padded = size + narrow + -(size + narrow) % 32
    send, keep = chain.run(
        "down_grad",
        lambda *args: down_grad_kernel(count, narrow, *args),
        [upstream, Fast(act), Fast(att_low), Fast(branch)],
        [Fast(sds((count // 2, padded, width), BF16))] * 2,
        [low, vmem((width, width), F32)],
    )
    down = Scatter(chain, "down", send, keep, count)
    chain.space()
    send, keep = chain.run(
        "up_value",
        lambda *args: up_value_kernel(heads, segs, count, *args),
        [weights, Fast(pre_grad), Fast(second), Fast(grads_turned)],
        [Fast(sds((count // 2, size + tokens, width), BF16))] * 2,
        [
            like(weights),
            vmem((heads, rows * HALF, span), BF16),
            vmem((rows, width, full), BF16),
            vmem((count, rows * width, span), BF16),
        ],
        meta=lengths,
    )
    up = Scatter(chain, "up", send, keep, count)
    chain.space("long_space")
    (shares,) = chain.run(
        "share_gate",
        share_kernel,
        [Fast(piece) for piece in shares],
        [sds((parts,) + shares[0].shape, BF16)],
    )
    down.step()
    up.step()

    (logit_part,) = chain.run(
        "logit",
        lambda *args: logit_kernel(each, segs, parts, count, *args),
        [weights, other_values, shares],
        [Fast(sds((chunks, each, span, CHUNK), BF16))],
        [
            vmem((rows * width, full + CHUNK), BF16),
            vmem((2, rows, WINDOW, CHUNK), BF16),
            vmem((2, each, rows * LANES, CHUNK), BF16),
            vmem((2, each, span, rows * LANES), BF16),
            vmem((chunks, each, span, CHUNK), F32),
            vmem((chunks, each, span, CHUNK), BF16),
            vmem(shares.shape, BF16),
            vmem((parts, 8, LANES), jnp.int32),
            pltpu.SMEM((parts, 8, LANES), jnp.int32),
        ],
        meta=lengths,
    )
    logit_grad = []

    def spread(pieces, place_of, picks=(0, 0), onward=0):
        results = chain.run(
            "spread",
            lambda *args: spread_kernel(len(pieces), place_of, picks, *args),
            [Fast(piece) for piece in pieces] + logit_grad,
            [sds((heads, span, full), F32)] + [Fast(sds(pieces[0].shape, BF16))] * onward,
            [vmem((each, span, full), F32)],
            copies=each,
            aliases={len(pieces): 0} if logit_grad else None,
        )
        logit_grad[:] = results[:1]
        return list(results[1:])

    def between(piece):
        return lax.ppermute(piece, "dp", [(1, 2), (2, 1)])

    def outward(piece):
        return lax.ppermute(piece, "dp", [(1, 0), (2, 3)])

    levels = count.bit_length() - 3
    if split:
        near_piece, far_piece = beside(logit_part, 1), between(logit_part)
        down.step(hold=True)
        spread([logit_part], lambda member: member)
    else:
        down.step(hold=True)
        spread([lax.psum(logit_part, "dp")], None)
    for unused in range(levels):
        up.step()
    if split:
        near_piece, far_piece = spread([near_piece, far_piece], lambda member: member ^ 1, (0, 0), 2)
        near_on, far_on = between(near_piece), outward(far_piece)
    layer_out = layer(chain, act, down_weight, hidden1, down_bias).reshape(rows, span, width)
    up, values_grad = up.last([size, tokens])
    up = Across(chain, "up", up, groups)
    down.release()
    for unused in range(levels - 1):
        down.step()
    down = Across(chain, "down", *down.last(), groups)

    extra_rows = n_small + 2
    extra_rows += -extra_rows % 16
    extra_rows += -(narrow + extra_rows) % 32
    input_grad, value_send, value_keep = chain.run(
        "tail",
        lambda *args: tail_kernel(heads, count, *args),
        [
            Fast(values_grad),
            inputs,
            first,
            hidden1_grad,
            ln1_gain,
            value_weight,
            small2,
        ],
        [sds((rows, span, width), F32)]
        + [Fast(sds((count // 2, narrow + extra_rows, width), BF16))] * 2,
        [like(inputs), low, bare, like(ln1_gain), like(value_weight), like(small2)]
        + [
            low,
            vmem((width, width), F32),
            vmem((extra_rows, width), F32),
            vmem((rows, span, width), F32),
        ],
    )
    value = Scatter(chain, "value", value_send, value_keep, count)
    if split:
        (near_on,) = spread(
            [far_piece, far_on, near_on], lambda member: 2 - member // 2, (1, 0), 1
        )
        near_out = outward(near_on)
    up.step()
    down.step()
    value.step()
    up.step()
    for unused in range(levels):
        value.step()
    if split:
        spread([near_on, near_out], lambda member: 3 - 3 * (member // 2), (1, 0))
    value = Across(chain, "value", *value.last(), groups)
    down.step()
    value.step()
    (up_weight_grad,) = up.finish(((size, True),))
    value.step()
    down_weight_grad, out_weight_grad = down.finish(((size, False), (narrow, False)))
    value_weight_grad, small = value.finish(((narrow, False), (extra_rows, False)))

    def mine(vector):
        length = vector.shape[0] // count
        return lax.dynamic_slice_in_dim(vector, here * length, length, 0)

    return (
        layer_out,
        input_grad,
        mine(small[0]),
        mine(small[1]),
        value_weight_grad,
        out_weight_grad,
        mine(small[5]),
        mine(small[3]),
        mine(small[4]),
        up_weight_grad,
        mine(small[6 : 6 + hidden_units // width].reshape(hidden_units)),
        down_weight_grad,
        mine(small[2]),
        logit_grad[0],
    )


def gate_kernel(meta, ins, outs, scratch, move):
    for source, target in zip(ins, outs):
        target[...] = source[...]


def gate(chain, name, arrays):
    return chain.run(
        name,
        gate_kernel,
        [Fast(array) for array in arrays],
        [Fast(sds(array.shape, array.dtype)) for array in arrays],
    )


def layer(chain, act, down_weight, hidden1, down_bias):
    (out,) = chain.run(
        "layer",
        layer_kernel,
        [act, down_weight, hidden1, down_bias],
        [sds(hidden1.shape, BF16)],
        [like(act), like(down_weight), like(hidden1), like(down_bias), like(hidden1, BF16)],
    )
    return out


def solution(mesh):
    return jax.shard_map(
        local,
        mesh=mesh,
        in_specs=(
            P("dp", "seq", None),
            P("dp", None),
            P(),
            P(),
            P(),
            P(),
            P(),
            P(),
            P(),
            P(),
            P(),
            P(),
            P(),
            P(None, "seq", None),
            P("dp", "seq", None),
        ),
        out_specs=(
            P("dp", "seq", None),
            P("dp", "seq", None),
            P("seq"),
            P("seq"),
            P("seq", None),
            P("seq", None),
            P("seq"),
            P("seq"),
            P("seq"),
            P(None, "seq"),
            P("seq"),
            P("seq", None),
            P("seq"),
            P(None, "seq", None),
        ),
        check_vma=False,
    )
```
